512 devices in a mesh: row: 16 (over z_hi, x, core), col: 32 (over z_lo, y).
Axes of the slice: x: 4, y: 4, z: 16 (z_hi: 2, z_lo: 8; z = z_hi * 8 + z_lo), core: 2. Of those that a mesh axis runs over, the one named last changes fastest.
Arguments:
- student: bfloat16 [65536, 768], P(('row', 'col')), may hold values from -0.21875 to 0.21875
- teacher: bfloat16 [65536, 768], P(('row', 'col')), may hold values from -32 to 32
Outputs:
- student_grad: float32 [65536, 768], P(('row', 'col'))
The draws below stay inside these ranges and needn't reach their ends.
All inputs are finite; a program needn't handle non-finite values.
Results may differ from the reference program's by a relative error of at most 0.0045.
Values may be sent and summed in bfloat16 or wider, within the bound.
No kernel may reach another device: no remote copies, remote signals or barrier semaphores. Data moves between devices by JAX's collectives and lax.ppermute only.
A program may use at most 64 MiB of HBM per device.

```python
import jax
import jax.numpy as jnp
from jax import lax

D = 768
BATCH = 4096
NTEXT = 65536
N_ROW = 16


def draw_teacher(key, part):
    key = jax.random.fold_in(key, 7)
    first, second = jax.random.split(key, 2)
    shared = jax.random.normal(first, (D,), jnp.float32)
    noise = jax.random.normal(second, (NTEXT, D), jnp.float32)
    batches = NTEXT // BATCH
    batch_id = (jnp.arange(NTEXT) // BATCH).astype(jnp.float32)
    level = batch_id / max(batches - 1, 1)
    share = 0.05 + 0.25 * level
    weight = jnp.sqrt(share / (1.0 - share))[:, None]
    values = jnp.clip(noise + weight * shared[None, :], -8.0, 8.0)
    return values.astype(jnp.bfloat16)


def steps_of(stream_key, shape, cuts, smallest, largest):
    def one(dim, parts):
        draws = jax.random.uniform(jax.random.fold_in(jax.random.fold_in(stream_key, 6), dim), (parts,), jnp.float32, smallest / len(cuts), largest / len(cuts))
        return jnp.repeat(jnp.exp(draws), shape[dim] // parts).reshape((-1,) + (1,) * (len(shape) - dim - 1))

    gain = one(*cuts[0])
    for cut in cuts[1:]:
        gain = gain * one(*cut)
    return gain


def normal_values(own_key, shape, deviation, most, pieces=(), kind=jnp.bfloat16):
    values = jax.random.normal(own_key, shape, jnp.float32) * deviation
    if len(pieces) > 0:
        values = steps_of(own_key, shape, pieces, -0.22, 0.18) * values
    return jnp.clip(values, min=-most, max=most).astype(kind)


def setup_inputs(seed: int = 0) -> dict:
    seeds = jax.random.split(jax.random.key(seed), 3)
    student = normal_values(seeds[0], (NTEXT, D), D ** -0.5, 0.21875, ((0, 512),))
    teacher = draw_teacher(jax.random.fold_in(seeds[2], 71), 0)
    return {"student": student, "teacher": teacher}


def unit_rows(values):
    wide = values.astype(jnp.float32)
    length = jnp.sqrt(lax.optimization_barrier(jnp.sum(wide * wide, axis=-1, keepdims=True)) + 1e-06)
    return (wide / length, length)

def reference(student, teacher):
    unit_f, norm_s = unit_rows(student)
    unit_s = unit_f.astype(jnp.bfloat16)
    unit_t = unit_rows(teacher)[0].astype(jnp.bfloat16)

    def one_batch(pair):
        rows_s, rows_t = pair
        student_gram = lax.dot_general(rows_s, rows_s, (((1,), (1,)), ((), ())), preferred_element_type=jnp.float32)
        teacher_gram = lax.dot_general(rows_t, rows_t, (((1,), (1,)), ((), ())), preferred_element_type=jnp.float32)
        mismatch = student_gram - teacher_gram
        pulled = jnp.dot(mismatch, rows_s.astype(jnp.float32), precision=lax.Precision.HIGHEST)
        return (pulled, jnp.sum(teacher_gram * teacher_gram))
    pulled, energies = lax.map(one_batch, (unit_s.reshape(N_ROW, BATCH, D), unit_t.reshape(N_ROW, BATCH, D)))
    energy = jnp.sum(energies)
    factor = BATCH ** 0.5 * NTEXT / energy
    pull = factor * pulled.reshape(NTEXT, D)
    along = lax.optimization_barrier(jnp.sum(pull * unit_f, axis=-1, keepdims=True))
    return (pull - along * unit_f) / norm_s
```

```python
import functools

import jax
import jax.numpy as jnp
from jax import lax
from jax.experimental import pallas as pl
from jax.experimental.pallas import tpu as pltpu
from jax.sharding import Mesh, PartitionSpec as P

NY = 4
NZ = 8
LANES = 128
TILE = 16
F32 = jnp.float32
BF16 = jnp.bfloat16
COL = ("zf", "z2", "z1", "y")
ALL = ("zh", "xc") + COL
VMEM_LIMIT = 12 * 1024 * 1024


def call(body, out_shape, operands, flops, scratch=(), after=()):
    size = sum(a.size * a.dtype.itemsize for a in operands)
    size += sum(s.size * s.dtype.itemsize for s in out_shape)
    count, extra = len(operands), len(after)

    def run(*refs):
        body(*refs[:count], *refs[count + extra :])

    whole = pl.BlockSpec(memory_space=pltpu.VMEM)
    return pl.pallas_call(
        run,
        out_shape=out_shape,
        in_specs=[whole] * count + [pl.BlockSpec(memory_space=pl.ANY)] * extra,
        out_specs=[whole] * len(out_shape),
        scratch_shapes=scratch,
        compiler_params=pltpu.CompilerParams(vmem_limit_bytes=VMEM_LIMIT),
        cost_estimate=pl.CostEstimate(flops=flops, bytes_accessed=size, transcendentals=0),
    )(*operands, *after)


def struct(shape, dtype):
    return jax.ShapeDtypeStruct(shape, dtype)


def unit_rows(values):
    wide = values.astype(F32)
    length = jnp.sqrt(jnp.sum(wide * wide, axis=-1, keepdims=True) + 1e-06)
    return (wide / length, length)


def split3(e):
    high = e.astype(BF16).astype(F32)
    mid = (e - high).astype(BF16).astype(F32)
    low = e - high - mid
    row = lax.broadcasted_iota(jnp.int32, (TILE, LANES), 0)
    parts = jnp.where(row == 0, high, jnp.where(row == 1, mid, jnp.where(row == 2, low, 0.0)))
    return parts.astype(BF16)


def join3(parts):
    return jnp.sum(parts.astype(F32), axis=0, keepdims=True)


def units_kernel(x_ref, copies_ref):
    unit = unit_rows(x_ref[...])[0].astype(BF16)
    for i in range(copies_ref.shape[0]):
        copies_ref[i] = unit


def nt(left, right):
    return lax.dot_general(left, right, (((1,), (1,)), ((), ())), preferred_element_type=F32)


def turned(ring_ref, flip):
    part = ring_ref.shape[1] // NY
    begin = lax.axis_index("y") * part // LANES * LANES
    rest = pl.multiple_of(lax.axis_index("y") * part - begin, TILE)
    flip[...] = ring_ref[:, pl.ds(pl.multiple_of(begin, LANES), 2 * LANES)].T
    return flip[pl.ds(rest, part)]


def split_rows(sums, axis, keep_ref, give_ref):
    rows = keep_ref.shape[0]
    here = lax.axis_index(axis)
    keep_ref[...] = sums[pl.ds(pl.multiple_of(here * rows, TILE), rows)]
    give_ref[...] = sums[pl.ds(pl.multiple_of((1 - here) * rows, TILE), rows)].astype(BF16)


def teacher_kernel(ring_ref, keep_ref, give_ref, flip, sums):
    sums[...] = jnp.dot(turned(ring_ref, flip), ring_ref[...], preferred_element_type=F32)
    split_rows(sums, "z1", keep_ref, give_ref)


def student_kernel(ring_s, ring_t, keep_ref, give_ref, flip, sums):
    width = ring_s.shape[1]
    part = sums.shape[0]
    left = turned(ring_s, flip)
    row = lax.broadcasted_iota(jnp.int32, (part, width), 0) + lax.axis_index("y") * part
    on = row == lax.broadcasted_iota(jnp.int32, (part, width), 1)
    sums[:, :width] = jnp.dot(left, ring_s[...], preferred_element_type=F32) - jnp.where(
        on, ring_s.shape[0] / width, 0.0
    )
    sums[:, width:] = -jnp.dot(left, ring_t[...], preferred_element_type=F32)
    split_rows(sums, "z1", keep_ref, give_ref)


def halve_kernel(mine_ref, got_ref, keep_ref, give_ref, sums):
    sums[...] = mine_ref[...] + got_ref[...].astype(F32)
    split_rows(sums, "z2", keep_ref, give_ref)


def energy_kernel(mine_ref, got_ref, e_ref):
    tt = mine_ref[...] + got_ref[...].astype(F32)
    e = jnp.sum(tt * tt, axis=0, keepdims=True)
    e = sum(e[:, i : i + LANES] for i in range(0, e.shape[1], LANES))
    e_ref[...] = jnp.broadcast_to(e, e_ref.shape)


def energies_kernel(e_ref, out_ref):
    out_ref[...] = jnp.sum(e_ref[...], axis=0)


def add_kernel(mine_ref, got_ref, total_ref, send_ref):
    total = mine_ref[...] + got_ref[...].astype(F32)
    total_ref[...] = total
    send_ref[...] = total.astype(BF16)


def exchange_kernel(mine_ref, got_ref, e_ref, f_ref, out_ref):
    main = mine_ref.shape[1]
    out_ref[:, :main] = (mine_ref[...] + got_ref[...].astype(F32)).astype(BF16)
    out_ref[:, main:] = jnp.zeros((out_ref.shape[0], LANES), BF16)
    out_ref[0:TILE, main:] = split3(e_ref[0:1] + f_ref[0:1])


def double_kernel(mine_ref, got_ref, out_ref):
    z2 = lax.axis_index("z2")
    rows, wide = mine_ref.shape
    main = wide - LANES
    out_ref[pl.ds(pl.multiple_of(z2 * rows, TILE), rows)] = mine_ref[...]
    out_ref[pl.ds(pl.multiple_of((1 - z2) * rows, TILE), rows)] = got_ref[...]
    e = join3(mine_ref[0:TILE, main:]) + join3(got_ref[0:TILE, main:])
    out_ref[0:TILE, main:] = split3(e)


def pull_kernel(mine_ref, got_ref, ring_s, ring_t, out_ref, whole):
    z1 = lax.axis_index("z1")
    rows, wide = mine_ref.shape
    main = wide - LANES
    whole[pl.ds(pl.multiple_of(z1 * rows, TILE), rows)] = mine_ref[:, :main]
    whole[pl.ds(pl.multiple_of((1 - z1) * rows, TILE), rows)] = got_ref[:, :main]
    width, part = main // 2, 2 * rows
    pull = nt(whole[:, :width], ring_s[...]) + nt(whole[:, width:], ring_t[...])
    e = join3(mine_ref[0:TILE, main:]) + join3(got_ref[0:TILE, main:])
    parts = split3(e)
    n = out_ref.shape[2]
    for i in range(NY):
        out_ref[i, 0:part] = pull[:, i * n : (i + 1) * n].astype(BF16)
        out_ref[i, part:] = parts


def finish_kernel(scale, diag, blocks_ref, student_ref, out_ref):
    n, width = student_ref.shape
    part = width // NY
    parts = sum(join3(blocks_ref[i, part:]) for i in range(NY))
    energy = jnp.sum(parts, axis=1, keepdims=True)
    factor = scale / energy
    unit_f, norm_s = unit_rows(student_ref[...])
    pull_t = jnp.concatenate([blocks_ref[i, 0:part].astype(F32) for i in range(NY)], axis=0)
    pull = (pull_t.T + diag * unit_f.astype(BF16).astype(F32)) * factor
    along = jnp.sum(pull * unit_f, axis=-1, keepdims=True)
    out_ref[...] = (pull - along * unit_f) / norm_s


def swap(x, axis):
    return lax.ppermute(x, axis, [(0, 1), (1, 0)])


def gather_y(x):
    n, width = x.shape
    (copies,) = call(units_kernel, [struct((NY, n, width), BF16)], [x], 5 * n * width)
    return lax.all_to_all(copies, "y", 0, 0).reshape(NY * n, width)


def on_device(student, teacher):
    n, width = student.shape
    batch_texts = n * lax.axis_size(COL)
    total_texts = n * lax.axis_size(ALL)
    part = width // NY
    half, rows = part // 2, part // 4
    texts = n * NY
    mac = texts * part * width

    def pair(rows, wide):
        return [struct((rows, wide), F32), struct((rows, wide), BF16)]

    def scratch(wide):
        return [pltpu.VMEM((2 * LANES, texts), BF16), pltpu.VMEM((part, wide), F32)]

    ring_t = gather_y(teacher)
    ring_s = gather_y(student)

    tt, tt_give = call(teacher_kernel, pair(half, width), [ring_t], 2 * mac, scratch(width))
    tt_got = swap(tt_give, "z1")
    tt, tt_give = call(
        halve_kernel, pair(rows, width), [tt, tt_got], part * width, [pltpu.VMEM((half, width), F32)]
    )
    tt_got = swap(tt_give, "z2")
    keep, give = call(
        student_kernel,
        pair(half, 2 * width),
        [ring_s, ring_t],
        4 * mac,
        scratch(2 * width),
        after=[tt_give],
    )
    got = swap(give, "z1")
    tt, tt_give = call(add_kernel, pair(rows, width), [tt, tt_got], rows * width)
    tt_got = swap(tt_give, "zf")
    keep, give = call(
        halve_kernel,
        pair(rows, 2 * width),
        [keep, got],
        2 * part * width,
        [pltpu.VMEM((half, 2 * width), F32)],
        after=[tt_give],
    )
    got = swap(give, "z2")
    near = lax.axis_size("xc")
    (e,) = call(
        energy_kernel,
        [struct((near, 8, LANES), F32)],
        [tt, tt_got],
        3 * rows * width,
        after=[give],
    )
    e = lax.all_to_all(e, "xc", 0, 0)
    keep, give = call(
        add_kernel, pair(rows, 2 * width), [keep, got], 2 * rows * width, after=[e]
    )
    got = swap(give, "zf")
    (e,) = call(energies_kernel, [struct((8, LANES), F32)], [e], e.size, after=[give])
    e_far = swap(e, "zh")
    (mine,) = call(
        exchange_kernel,
        [struct((rows, 2 * width + LANES), BF16)],
        [keep, got, e, e_far],
        2 * rows * width,
    )
    got = swap(mine, "z2")
    (mine,) = call(
        double_kernel, [struct((half, 2 * width + LANES), BF16)], [mine, got], 2 * rows * width
    )
    got = swap(mine, "z1")
    (blocks,) = call(
        pull_kernel,
        [struct((NY, part + TILE, n), BF16)],
        [mine, got, ring_s, ring_t],
        4 * mac,
        [pltpu.VMEM((part, 2 * width), BF16)],
    )
    blocks = lax.all_to_all(blocks, "y", 0, 0)
    (out,) = call(
        functools.partial(finish_kernel, batch_texts**0.5 * total_texts, batch_texts / width),
        [struct((n, width), F32)],
        [blocks, student],
        12 * n * width,
    )
    return out


def solution(mesh):
    rows, cols = mesh.devices.shape
    fine = Mesh(mesh.devices.reshape(2, rows // 2, 2, 2, 2, cols // NZ), ALL)
    return jax.shard_map(
        on_device,
        mesh=fine,
        in_specs=(P(ALL, None), P(ALL, None)),
        out_specs=P(ALL, None),
        check_vma=False,
    )
```

```python
import functools

import jax
import jax.numpy as jnp
from jax import lax
from jax.experimental import pallas as pl
from jax.experimental.pallas import tpu as pltpu
from jax.sharding import Mesh, PartitionSpec as P

NY = 4
NZ = 8
LANES = 128
TILE = 16
F32 = jnp.float32
BF16 = jnp.bfloat16
COL = ("zf", "z2", "z1", "y")
ALL = ("zh", "xc") + COL
VMEM_LIMIT = 12 * 1024 * 1024


def call(body, out_shape, operands, flops, scratch=(), after=()):
    size = sum(a.size * a.dtype.itemsize for a in operands)
    size += sum(s.size * s.dtype.itemsize for s in out_shape)
    count, extra = len(operands), len(after)

    def run(*refs):
        body(*refs[:count], *refs[count + extra :])

    whole = pl.BlockSpec(memory_space=pltpu.VMEM)
    return pl.pallas_call(
        run,
        out_shape=out_shape,
        in_specs=[whole] * count + [pl.BlockSpec(memory_space=pl.ANY)] * extra,
        out_specs=[whole] * len(out_shape),
        scratch_shapes=scratch,
        compiler_params=pltpu.CompilerParams(vmem_limit_bytes=VMEM_LIMIT),
        cost_estimate=pl.CostEstimate(flops=flops, bytes_accessed=size, transcendentals=0),
    )(*operands, *after)


def struct(shape, dtype):
    return jax.ShapeDtypeStruct(shape, dtype)


def unit_rows(values):
    wide = values.astype(F32)
    length = jnp.sqrt(jnp.sum(wide * wide, axis=-1, keepdims=True) + 1e-06)
    return (wide / length, length)


def split3(e):
    high = e.astype(BF16).astype(F32)
    mid = (e - high).astype(BF16).astype(F32)
    low = e - high - mid
    row = lax.broadcasted_iota(jnp.int32, (TILE, LANES), 0)
    parts = jnp.where(row == 0, high, jnp.where(row == 1, mid, jnp.where(row == 2, low, 0.0)))
    return parts.astype(BF16)


def join3(parts):
    return jnp.sum(parts.astype(F32), axis=0, keepdims=True)


def units_kernel(x_ref, copies_ref):
    unit = unit_rows(x_ref[...])[0].astype(BF16)
    for i in range(copies_ref.shape[0]):
        copies_ref[i] = unit


def nt(left, right):
    return lax.dot_general(left, right, (((1,), (1,)), ((), ())), preferred_element_type=F32)


def turned(ring_ref, flip):
    part = ring_ref.shape[1] // NY
    begin = lax.axis_index("y") * part // LANES * LANES
    rest = pl.multiple_of(lax.axis_index("y") * part - begin, TILE)
    flip[...] = ring_ref[:, pl.ds(pl.multiple_of(begin, LANES), 2 * LANES)].T
    return flip[pl.ds(rest, part)]


def split_rows(sums, axis, keep_ref, give_ref):
    rows = keep_ref.shape[0]
    here = lax.axis_index(axis)
    keep_ref[...] = sums[pl.ds(pl.multiple_of(here * rows, TILE), rows)]
    give_ref[...] = sums[pl.ds(pl.multiple_of((1 - here) * rows, TILE), rows)].astype(BF16)


def teacher_kernel(ring_ref, keep_ref, give_ref, flip, sums):
    sums[...] = jnp.dot(turned(ring_ref, flip), ring_ref[...], preferred_element_type=F32)
    split_rows(sums, "z1", keep_ref, give_ref)


def student_kernel(ring_s, ring_t, give_ref, flip):
    width = ring_s.shape[1]
    quad, rows = give_ref.shape[:2]
    part = quad * rows
    left = turned(ring_s, flip)
    row = lax.broadcasted_iota(jnp.int32, (part, width), 0) + lax.axis_index("y") * part
    on = row == lax.broadcasted_iota(jnp.int32, (part, width), 1)
    ss = jnp.dot(left, ring_s[...], preferred_element_type=F32)
    ss = (ss - jnp.where(on, ring_s.shape[0] / width, 0.0)).astype(BF16)
    st = -jnp.dot(left, ring_t[...], preferred_element_type=F32).astype(BF16)
    for i in range(quad):
        give_ref[i, :, :width] = ss[i * rows : (i + 1) * rows]
        give_ref[i, :, width:] = st[i * rows : (i + 1) * rows]


def quad_kernel(got_ref, total_ref, send_ref):
    total = jnp.sum(got_ref[...].astype(F32), axis=0)
    total_ref[...] = total
    send_ref[...] = total.astype(BF16)


def halve_kernel(mine_ref, got_ref, keep_ref, give_ref, sums):
    sums[...] = mine_ref[...] + got_ref[...].astype(F32)
    split_rows(sums, "z2", keep_ref, give_ref)


def energy_kernel(mine_ref, got_ref, e_ref):
    tt = mine_ref[...] + got_ref[...].astype(F32)
    e = jnp.sum(tt * tt, axis=0, keepdims=True)
    e = sum(e[:, i : i + LANES] for i in range(0, e.shape[1], LANES))
    e_ref[...] = jnp.broadcast_to(e, e_ref.shape)


def energies_kernel(e_ref, out_ref):
    out_ref[...] = jnp.broadcast_to(jnp.sum(e_ref[...], axis=0), out_ref.shape)


def add_kernel(mine_ref, got_ref, total_ref, send_ref):
    total = mine_ref[...] + got_ref[...].astype(F32)
    total_ref[...] = total
    send_ref[...] = total.astype(BF16)


def exchange_kernel(mine_ref, got_ref, out_ref):
    out_ref[...] = jnp.broadcast_to(
        (mine_ref[...] + got_ref[...].astype(F32)).astype(BF16), out_ref.shape
    )


def pull_kernel(whole, ring_s, ring_t, e_ref, f_ref, out_ref):
    part, width = whole.shape[0], whole.shape[1] // 2
    pull = nt(whole[:, :width], ring_s[...]) + nt(whole[:, width:], ring_t[...])
    parts = split3(e_ref[0:1] + f_ref[0:1])
    n = out_ref.shape[2]
    for i in range(NY):
        out_ref[i, 0:part] = pull[:, i * n : (i + 1) * n].astype(BF16)
        out_ref[i, part:] = parts


def finish_kernel(scale, diag, blocks_ref, student_ref, out_ref):
    n, width = student_ref.shape
    part = width // NY
    parts = sum(join3(blocks_ref[i, part:]) for i in range(NY))
    energy = jnp.sum(parts, axis=1, keepdims=True)
    factor = scale / energy
    unit_f, norm_s = unit_rows(student_ref[...])
    pull_t = jnp.concatenate([blocks_ref[i, 0:part].astype(F32) for i in range(NY)], axis=0)
    pull = (pull_t.T + diag * unit_f.astype(BF16).astype(F32)) * factor
    along = jnp.sum(pull * unit_f, axis=-1, keepdims=True)
    out_ref[...] = (pull - along * unit_f) / norm_s


def swap(x, axis):
    return lax.ppermute(x, axis, [(0, 1), (1, 0)])


def gather_y(x):
    n, width = x.shape
    (copies,) = call(units_kernel, [struct((NY, n, width), BF16)], [x], 5 * n * width)
    return lax.all_to_all(copies, "y", 0, 0).reshape(NY * n, width)


def on_device(student, teacher):
    n, width = student.shape
    batch_texts = n * lax.axis_size(COL)
    total_texts = n * lax.axis_size(ALL)
    part = width // NY
    half, rows = part // 2, part // 4
    texts = n * NY
    mac = texts * part * width

    def pair(rows, wide):
        return [struct((rows, wide), F32), struct((rows, wide), BF16)]

    def scratch(wide):
        return [pltpu.VMEM((2 * LANES, texts), BF16), pltpu.VMEM((part, wide), F32)]

    ring_t = gather_y(teacher)
    ring_s = gather_y(student)

    quad = ("z2", "z1")
    tt, tt_give = call(teacher_kernel, pair(half, width), [ring_t], 2 * mac, scratch(width))
    tt_got = swap(tt_give, "z1")
    tt, tt_give = call(
        halve_kernel, pair(rows, width), [tt, tt_got], part * width, [pltpu.VMEM((half, width), F32)]
    )
    tt_got = swap(tt_give, "z2")
    tt, tt_give = call(add_kernel, pair(rows, width), [tt, tt_got], rows * width)
    tt_got = swap(tt_give, "zf")
    (give,) = call(
        student_kernel,
        [struct((4, rows, 2 * width), BF16)],
        [ring_s, ring_t],
        4 * mac,
        [pltpu.VMEM((2 * LANES, texts), BF16)],
        after=[tt_give],
    )
    got = lax.all_to_all(give, quad, 0, 0)
    keep, give = call(
        quad_kernel, pair(rows, 2 * width), [got], 4 * rows * width, after=[tt_got]
    )
    got = swap(give, "zf")
    some = ("xc", "z2", "z1")
    (e,) = call(
        energy_kernel,
        [struct((lax.axis_size(some), 1, LANES), F32)],
        [tt, tt_got],
        3 * rows * width,
        after=[give],
    )
    e = lax.all_to_all(e, some, 0, 0)
    (mine,) = call(
        exchange_kernel,
        [struct((4, rows, 2 * width), BF16)],
        [keep, got],
        2 * rows * width,
        after=[e],
    )
    whole = lax.all_to_all(mine, quad, 0, 0).reshape(part, 2 * width)
    (e,) = call(energies_kernel, [struct((8, LANES), F32)], [e], e.size, after=[mine])
    e_far = swap(e, "zh")
    (blocks,) = call(
        pull_kernel,
        [struct((NY, part + TILE, n), BF16)],
        [whole, ring_s, ring_t, e, e_far],
        4 * mac,
    )
    blocks = lax.all_to_all(blocks, "y", 0, 0)
    (out,) = call(
        functools.partial(finish_kernel, batch_texts**0.5 * total_texts, batch_texts / width),
        [struct((n, width), F32)],
        [blocks, student],
        12 * n * width,
    )
    return out


def solution(mesh):
    rows, cols = mesh.devices.shape
    fine = Mesh(mesh.devices.reshape(2, rows // 2, 2, 2, 2, cols // NZ), ALL)
    return jax.shard_map(
        on_device,
        mesh=fine,
        in_specs=(P(ALL, None), P(ALL, None)),
        out_specs=P(ALL, None),
        check_vma=False,
    )
```

```python
import functools

import jax
import jax.numpy as jnp
from jax import lax
from jax.experimental import pallas as pl
from jax.experimental.pallas import tpu as pltpu
from jax.sharding import Mesh, PartitionSpec as P

NY = 4
NZ = 8
LANES = 128
TILE = 16
F32 = jnp.float32
BF16 = jnp.bfloat16
COL = ("zf", "z2", "z1", "y")
ALL = ("zh", "xc") + COL
VMEM_LIMIT = 12 * 1024 * 1024


def call(body, out_shape, operands, flops, scratch=(), after=()):
    size = sum(a.size * a.dtype.itemsize for a in operands)
    size += sum(s.size * s.dtype.itemsize for s in out_shape)
    count, extra = len(operands), len(after)

    def run(*refs):
        body(*refs[:count], *refs[count + extra :])

    whole = pl.BlockSpec(memory_space=pltpu.VMEM)
    return pl.pallas_call(
        run,
        out_shape=out_shape,
        in_specs=[whole] * count + [pl.BlockSpec(memory_space=pl.ANY)] * extra,
        out_specs=[whole] * len(out_shape),
        scratch_shapes=scratch,
        compiler_params=pltpu.CompilerParams(vmem_limit_bytes=VMEM_LIMIT),
        cost_estimate=pl.CostEstimate(flops=flops, bytes_accessed=size, transcendentals=0),
    )(*operands, *after)


def struct(shape, dtype):
    return jax.ShapeDtypeStruct(shape, dtype)


def unit_rows(values):
    wide = values.astype(F32)
    length = jnp.sqrt(jnp.sum(wide * wide, axis=-1, keepdims=True) + 1e-06)
    return (wide / length, length)


def split3(e):
    high = e.astype(BF16).astype(F32)
    mid = (e - high).astype(BF16).astype(F32)
    low = e - high - mid
    row = lax.broadcasted_iota(jnp.int32, (TILE, LANES), 0)
    parts = jnp.where(row == 0, high, jnp.where(row == 1, mid, jnp.where(row == 2, low, 0.0)))
    return parts.astype(BF16)


def join3(parts):
    return jnp.sum(parts.astype(F32), axis=0, keepdims=True)


def units_kernel(s_ref, t_ref, own_ref):
    width = s_ref.shape[1]
    own_ref[:, :width] = unit_rows(s_ref[...])[0].astype(BF16)
    own_ref[:, width:] = unit_rows(t_ref[...])[0].astype(BF16)


def nt(left, right):
    return lax.dot_general(left, right, (((1,), (1,)), ((), ())), preferred_element_type=F32)


def turned(ring_ref, at, part, flip):
    begin = lax.axis_index("y") * part // LANES * LANES
    rest = pl.multiple_of(lax.axis_index("y") * part - begin, TILE)
    flip[...] = ring_ref[:, pl.ds(pl.multiple_of(at + begin, LANES), 2 * LANES)].T
    return flip[pl.ds(rest, part)]


def products_kernel(own, prev, following, top, bottom, ring_ref, give_ref, flip):
    n, width = own.shape[0], own.shape[1] // 2
    y = lax.axis_index("y")
    for d, at, ref in ((0, 0, own), (3, 0, prev), (1, 0, following), (2, 0, top), (2, n // 2, bottom)):
        begin = pl.multiple_of(lax.rem(y + d, NY) * n + at, n // 2)
        ring_ref[pl.ds(begin, ref.shape[0])] = ref[...]
    quad, rows = give_ref.shape[:2]
    part = quad * rows
    left = turned(ring_ref, 0, part, flip)
    ss = jnp.dot(left, ring_ref[:, :width], preferred_element_type=F32)
    row = lax.broadcasted_iota(jnp.int32, (part, width), 0) + y * part
    on = row == lax.broadcasted_iota(jnp.int32, (part, width), 1)
    ss = ss - jnp.where(on, NY * n / width, 0.0)
    st = -jnp.dot(left, ring_ref[:, width:], preferred_element_type=F32)
    left = turned(ring_ref, width, part, flip)
    tt = jnp.dot(left, ring_ref[:, width:], preferred_element_type=F32)
    for at, sums in ((0, ss), (width, st), (2 * width, tt)):
        for i in range(quad):
            give_ref[i, :, at : at + width] = sums[i * rows : (i + 1) * rows].astype(BF16)


def quad_kernel(got_ref, *refs):
    total = jnp.sum(got_ref[...].astype(F32), axis=0)
    at = 0
    for total_ref, send_ref in (refs[:2], refs[2:]):
        piece = total[:, at : at + total_ref.shape[1]]
        total_ref[...] = piece
        send_ref[...] = piece.astype(BF16)
        at += total_ref.shape[1]


def energy_kernel(mine_ref, got_ref, e_ref):
    tt = mine_ref[...] + got_ref[...].astype(F32)
    e = jnp.sum(tt * tt, axis=0, keepdims=True)
    e = sum(e[:, i : i + LANES] for i in range(0, e.shape[1], LANES))
    e_ref[...] = jnp.broadcast_to(e, e_ref.shape)


def energies_kernel(e_ref, out_ref):
    out_ref[...] = jnp.broadcast_to(jnp.sum(e_ref[...], axis=0), out_ref.shape)


def exchange_kernel(mine_ref, got_ref, out_ref):
    total = (mine_ref[...] + got_ref[...].astype(F32)).astype(BF16)
    for i in range(out_ref.shape[0]):
        out_ref[i] = total


def pull_kernel(whole, ring_ref, e_ref, f_ref, out_ref):
    part, n = whole.shape[0], out_ref.shape[2]
    pull = nt(whole[...], ring_ref[...])
    parts = split3(e_ref[0:1] + f_ref[0:1])
    for i in range(NY):
        out_ref[i, 0:part] = pull[:, i * n : (i + 1) * n].astype(BF16)
        out_ref[i, part:] = parts


def finish_kernel(scale, diag, blocks_ref, student_ref, out_ref):
    n, width = student_ref.shape
    part = width // NY
    parts = sum(join3(blocks_ref[i, part:]) for i in range(NY))
    energy = jnp.sum(parts, axis=1, keepdims=True)
    factor = scale / energy
    unit_f, norm_s = unit_rows(student_ref[...])
    pull_t = jnp.concatenate([blocks_ref[i, 0:part].astype(F32) for i in range(NY)], axis=0)
    pull = (pull_t.T + diag * unit_f.astype(BF16).astype(F32)) * factor
    along = jnp.sum(pull * unit_f, axis=-1, keepdims=True)
    out_ref[...] = (pull - along * unit_f) / norm_s


def swap(x, axis):
    return lax.ppermute(x, axis, [(0, 1), (1, 0)])


def shift_y(x, d):
    return lax.ppermute(x, "y", [(i, (i + d) % NY) for i in range(NY)])


def on_device(student, teacher):
    n, width = student.shape
    batch_texts = n * lax.axis_size(COL)
    total_texts = n * lax.axis_size(ALL)
    part = width // NY
    rows = part // 4
    texts = n * NY
    mac = texts * part * width
    quad = ("z2", "z1")

    def pair(wide):
        return [struct((rows, wide), F32), struct((rows, wide), BF16)]

    (own,) = call(units_kernel, [struct((n, 2 * width), BF16)], [student, teacher], 10 * n * width)
    prev = shift_y(own, 1)
    following = shift_y(own, -1)
    top = shift_y(prev[: n // 2], 1)
    bottom = shift_y(following[n // 2 :], -1)

    ring, give = call(
        products_kernel,
        [struct((texts, 2 * width), BF16), struct((4, rows, 3 * width), BF16)],
        [own, prev, following, top, bottom],
        6 * mac,
        [pltpu.VMEM((2 * LANES, texts), BF16)],
    )
    got = lax.all_to_all(give, quad, 0, 0)
    keep, give, tt, tt_give = call(
        quad_kernel, pair(2 * width) + pair(width), [got], 3 * part * width
    )
    tt_got = swap(tt_give, "zf")
    got = swap(give, "zf")
    some = ("xc", "z2", "z1")
    (e,) = call(
        energy_kernel,
        [struct((lax.axis_size(some), 1, LANES), F32)],
        [tt, tt_got],
        3 * rows * width,
    )
    e = lax.all_to_all(e, some, 0, 0)
    (mine,) = call(
        exchange_kernel,
        [struct((4, rows, 2 * width), BF16)],
        [keep, got],
        2 * rows * width,
        after=[e],
    )
    whole = lax.all_to_all(mine, quad, 0, 0).reshape(part, 2 * width)
    (e,) = call(energies_kernel, [struct((8, LANES), F32)], [e], e.size, after=[mine])
    e_far = swap(e, "zh")
    (blocks,) = call(
        pull_kernel,
        [struct((NY, part + TILE, n), BF16)],
        [whole, ring, e, e_far],
        4 * mac,
    )
    blocks = lax.all_to_all(blocks, "y", 0, 0)
    (out,) = call(
        functools.partial(finish_kernel, batch_texts**0.5 * total_texts, batch_texts / width),
        [struct((n, width), F32)],
        [blocks, student],
        12 * n * width,
    )
    return out


def solution(mesh):
    rows, cols = mesh.devices.shape
    fine = Mesh(mesh.devices.reshape(2, rows // 2, 2, 2, 2, cols // NZ), ALL)
    return jax.shard_map(
        on_device,
        mesh=fine,
        in_specs=(P(ALL, None), P(ALL, None)),
        out_specs=P(ALL, None),
        check_vma=False,
    )
```

```python
import functools

import jax
import jax.numpy as jnp
from jax import lax
from jax.experimental import pallas as pl
from jax.experimental.pallas import tpu as pltpu
from jax.sharding import Mesh, PartitionSpec as P

NY = 4
NZ = 8
LANES = 128
TILE = 16
F32 = jnp.float32
BF16 = jnp.bfloat16
COL = ("zf", "z2", "z1", "y")
ALL = ("zh", "xc") + COL
VMEM_LIMIT = 12 * 1024 * 1024


def call(body, out_shape, operands, flops, scratch=(), after=()):
    size = sum(a.size * a.dtype.itemsize for a in operands)
    size += sum(s.size * s.dtype.itemsize for s in out_shape)
    count, extra = len(operands), len(after)

    def run(*refs):
        body(*refs[:count], *refs[count + extra :])

    whole = pl.BlockSpec(memory_space=pltpu.VMEM)
    return pl.pallas_call(
        run,
        out_shape=out_shape,
        in_specs=[whole] * count + [pl.BlockSpec(memory_space=pl.ANY)] * extra,
        out_specs=[whole] * len(out_shape),
        scratch_shapes=scratch,
        compiler_params=pltpu.CompilerParams(vmem_limit_bytes=VMEM_LIMIT),
        cost_estimate=pl.CostEstimate(flops=flops, bytes_accessed=size, transcendentals=0),
    )(*operands, *after)


def struct(shape, dtype):
    return jax.ShapeDtypeStruct(shape, dtype)


def unit_rows(values):
    wide = values.astype(F32)
    length = jnp.sqrt(jnp.sum(wide * wide, axis=-1, keepdims=True) + 1e-06)
    return (wide / length, length)


def split3(e):
    high = e.astype(BF16).astype(F32)
    mid = (e - high).astype(BF16).astype(F32)
    low = e - high - mid
    row = lax.broadcasted_iota(jnp.int32, (TILE, LANES), 0)
    parts = jnp.where(row == 0, high, jnp.where(row == 1, mid, jnp.where(row == 2, low, 0.0)))
    return parts.astype(BF16)


def join3(parts):
    return jnp.sum(parts.astype(F32), axis=0, keepdims=True)


def units_kernel(x_ref, unit_ref):
    unit_ref[...] = jnp.broadcast_to(unit_rows(x_ref[...])[0].astype(BF16), unit_ref.shape)


def nt(left, right):
    return lax.dot_general(left, right, (((1,), (1,)), ((), ())), preferred_element_type=F32)


def turned(ring_ref, flip):
    part = ring_ref.shape[1] // NY
    begin = lax.axis_index("y") * part // LANES * LANES
    rest = pl.multiple_of(lax.axis_index("y") * part - begin, TILE)
    flip[...] = ring_ref[:, pl.ds(pl.multiple_of(begin, LANES), 2 * LANES)].T
    return flip[pl.ds(rest, part)]


def split_rows(sums, axis, keep_ref, give_ref):
    rows = keep_ref.shape[0]
    here = lax.axis_index(axis)
    keep_ref[...] = sums[pl.ds(pl.multiple_of(here * rows, TILE), rows)]
    give_ref[...] = sums[pl.ds(pl.multiple_of((1 - here) * rows, TILE), rows)].astype(BF16)


def teacher_kernel(ring_ref, keep_ref, give_ref, flip, upper):
    y = lax.axis_index("y")
    count = ring_ref.shape[1] // LANES
    for i, block in ((0, y), (1, jnp.minimum(count - y, count - 1))):
        begin = pl.multiple_of(block * LANES, LANES)
        flip[i * LANES : (i + 1) * LANES] = ring_ref[:, pl.ds(begin, LANES)].T
    for k in range(count):
        first = k < count - y
        row_block = jnp.where(first, y, count - y)
        col_block = jnp.where(first, y + k, k)
        used = jnp.logical_or(first, 2 * y < count)
        col_block = jnp.where(used, col_block, 0)
        weight = jnp.where(used, jnp.where(row_block == col_block, 1.0, 2.0**0.5), 0.0)
        left = flip[pl.ds(pl.multiple_of(jnp.where(first, 0, LANES), LANES), LANES)]
        right = ring_ref[:, pl.ds(pl.multiple_of(col_block * LANES, LANES), LANES)]
        block = jnp.dot(left, right, preferred_element_type=F32)
        upper[k * LANES : (k + 1) * LANES] = weight * block
    split_rows(upper, "z1", keep_ref, give_ref)


def student_kernel(ring_s, ring_t, give_ref, flip):
    width = ring_s.shape[1]
    quad, rows = give_ref.shape[:2]
    part = quad * rows
    left = turned(ring_s, flip)
    ss = jnp.dot(left, ring_s[...], preferred_element_type=F32)
    row = lax.broadcasted_iota(jnp.int32, (part, width), 0) + lax.axis_index("y") * part
    on = row == lax.broadcasted_iota(jnp.int32, (part, width), 1)
    ss = ss - jnp.where(on, ring_s.shape[0] / width, 0.0)
    st = -jnp.dot(left, ring_t[...], preferred_element_type=F32)
    for at, sums in ((0, ss), (width, st)):
        for i in range(quad):
            give_ref[i, :, at : at + width] = sums[i * rows : (i + 1) * rows].astype(BF16)


def quad_kernel(got_ref, total_ref, send_ref):
    total = jnp.sum(got_ref[...].astype(F32), axis=0)
    total_ref[...] = total
    send_ref[...] = total.astype(BF16)


def halve_kernel(mine_ref, got_ref, keep_ref, give_ref, sums):
    sums[...] = mine_ref[...] + got_ref[...].astype(F32)
    split_rows(sums, "z2", keep_ref, give_ref)


def energy_kernel(mine_ref, got_ref, e_ref):
    tt = mine_ref[...] + got_ref[...].astype(F32)
    e_ref[...] = jnp.broadcast_to(jnp.sum(tt * tt, axis=0, keepdims=True), e_ref.shape)


def energies_kernel(e_ref, out_ref):
    out_ref[...] = jnp.broadcast_to(jnp.sum(e_ref[...], axis=0), out_ref.shape)


def add_kernel(mine_ref, got_ref, total_ref, send_ref):
    total = mine_ref[...] + got_ref[...].astype(F32)
    total_ref[...] = total
    send_ref[...] = total.astype(BF16)


def exchange_kernel(mine_ref, got_ref, out_ref):
    out_ref[...] = jnp.broadcast_to(
        (mine_ref[...] + got_ref[...].astype(F32)).astype(BF16), out_ref.shape
    )


def pull_kernel(whole, ring_s, ring_t, e_ref, f_ref, out_ref):
    part, width = whole.shape[0], whole.shape[1] // 2
    pull = nt(whole[:, :width], ring_s[...]) + nt(whole[:, width:], ring_t[...])
    parts = split3(e_ref[0:1] + f_ref[0:1])
    n = out_ref.shape[2]
    for i in range(NY):
        out_ref[i, 0:part] = pull[:, i * n : (i + 1) * n].astype(BF16)
        out_ref[i, part:] = parts


def finish_kernel(scale, diag, blocks_ref, student_ref, out_ref):
    n, width = student_ref.shape
    part = width // NY
    parts = sum(join3(blocks_ref[i, part:]) for i in range(NY))
    energy = jnp.sum(parts, axis=1, keepdims=True)
    factor = scale / energy
    unit_f, norm_s = unit_rows(student_ref[...])
    pull_t = jnp.concatenate([blocks_ref[i, 0:part].astype(F32) for i in range(NY)], axis=0)
    pull = (pull_t.T + diag * unit_f.astype(BF16).astype(F32)) * factor
    along = jnp.sum(pull * unit_f, axis=-1, keepdims=True)
    out_ref[...] = (pull - along * unit_f) / norm_s


def swap(x, axis):
    return lax.ppermute(x, axis, [(0, 1), (1, 0)])


def gather_y(x):
    n, width = x.shape
    (copies,) = call(units_kernel, [struct((NY, n, width), BF16)], [x], 5 * n * width)
    return lax.all_to_all(copies, "y", 0, 0).reshape(NY * n, width)


def on_device(student, teacher):
    n, width = student.shape
    batch_texts = n * lax.axis_size(COL)
    total_texts = n * lax.axis_size(ALL)
    part = width // NY
    half, rows = part // 2, part // 4
    texts = n * NY
    mac = texts * part * width

    def pair(rows, wide):
        return [struct((rows, wide), F32), struct((rows, wide), BF16)]

    def scratch(wide):
        return [pltpu.VMEM((2 * LANES, texts), BF16), pltpu.VMEM((part, wide), F32)]

    ring_t = gather_y(teacher)
    ring_s = gather_y(student)

    quad = ("z2", "z1")
    tt, tt_give = call(
        teacher_kernel,
        pair(width // 2, LANES),
        [ring_t],
        mac,
        [pltpu.VMEM((2 * LANES, texts), BF16), pltpu.VMEM((width, LANES), F32)],
    )
    tt_got = swap(tt_give, "z1")
    tt, tt_give = call(
        halve_kernel,
        pair(width // 4, LANES),
        [tt, tt_got],
        part * width,
        [pltpu.VMEM((width // 2, LANES), F32)],
    )
    tt_got = swap(tt_give, "z2")
    tt, tt_give = call(add_kernel, pair(width // 4, LANES), [tt, tt_got], rows * width)
    tt_got = swap(tt_give, "zf")
    (give,) = call(
        student_kernel,
        [struct((4, rows, 2 * width), BF16)],
        [ring_s, ring_t],
        4 * mac,
        [pltpu.VMEM((2 * LANES, texts), BF16)],
        after=[tt_give],
    )
    got = lax.all_to_all(give, quad, 0, 0)
    keep, give = call(
        quad_kernel, pair(rows, 2 * width), [got], 4 * rows * width, after=[tt_got]
    )
    got = swap(give, "zf")
    some = ("xc", "z2", "z1")
    (e,) = call(
        energy_kernel,
        [struct((lax.axis_size(some), 1, LANES), F32)],
        [tt, tt_got],
        3 * rows * width,
        after=[give],
    )
    e = lax.all_to_all(e, some, 0, 0)
    (mine,) = call(
        exchange_kernel,
        [struct((4, rows, 2 * width), BF16)],
        [keep, got],
        2 * rows * width,
        after=[e],
    )
    whole = lax.all_to_all(mine, quad, 0, 0).reshape(part, 2 * width)
    (e,) = call(energies_kernel, [struct((8, LANES), F32)], [e], e.size, after=[mine])
    e_far = swap(e, "zh")
    (blocks,) = call(
        pull_kernel,
        [struct((NY, part + TILE, n), BF16)],
        [whole, ring_s, ring_t, e, e_far],
        4 * mac,
    )
    blocks = lax.all_to_all(blocks, "y", 0, 0)
    (out,) = call(
        functools.partial(finish_kernel, batch_texts**0.5 * total_texts, batch_texts / width),
        [struct((n, width), F32)],
        [blocks, student],
        12 * n * width,
    )
    return out


def solution(mesh):
    rows, cols = mesh.devices.shape
    fine = Mesh(mesh.devices.reshape(2, rows // 2, 2, 2, 2, cols // NZ), ALL)
    return jax.shard_map(
        on_device,
        mesh=fine,
        in_specs=(P(ALL, None), P(ALL, None)),
        out_specs=P(ALL, None),
        check_vma=False,
    )
```

```python
import functools

import jax
import jax.numpy as jnp
from jax import lax
from jax.experimental import pallas as pl
from jax.experimental.pallas import tpu as pltpu
from jax.sharding import Mesh, PartitionSpec as P

NY = 4
NZ = 8
LANES = 128
TILE = 16
F32 = jnp.float32
BF16 = jnp.bfloat16
COL = ("zf", "z2", "z1", "y")
ALL = ("zh", "xc") + COL
VMEM_LIMIT = 12 * 1024 * 1024


def call(body, out_shape, operands, flops, scratch=(), after=()):
    size = sum(a.size * a.dtype.itemsize for a in operands)
    size += sum(s.size * s.dtype.itemsize for s in out_shape)
    count, extra = len(operands), len(after)

    def run(*refs):
        body(*refs[:count], *refs[count + extra :])

    whole = pl.BlockSpec(memory_space=pltpu.VMEM)
    return pl.pallas_call(
        run,
        out_shape=out_shape,
        in_specs=[whole] * count + [pl.BlockSpec(memory_space=pl.ANY)] * extra,
        out_specs=[whole] * len(out_shape),
        scratch_shapes=scratch,
        compiler_params=pltpu.CompilerParams(vmem_limit_bytes=VMEM_LIMIT),
        cost_estimate=pl.CostEstimate(flops=flops, bytes_accessed=size, transcendentals=0),
    )(*operands, *after)


def struct(shape, dtype):
    return jax.ShapeDtypeStruct(shape, dtype)


def unit_rows(values):
    wide = values.astype(F32)
    length = jnp.sqrt(jnp.sum(wide * wide, axis=-1, keepdims=True) + 1e-06)
    return (wide / length, length)


def split3(e):
    high = e.astype(BF16).astype(F32)
    mid = (e - high).astype(BF16).astype(F32)
    low = e - high - mid
    row = lax.broadcasted_iota(jnp.int32, (TILE, LANES), 0)
    parts = jnp.where(row == 0, high, jnp.where(row == 1, mid, jnp.where(row == 2, low, 0.0)))
    return parts.astype(BF16)


def join3(parts):
    return jnp.sum(parts.astype(F32), axis=0, keepdims=True)


def units_kernel(x_ref, unit_ref):
    unit_ref[...] = jnp.broadcast_to(unit_rows(x_ref[...])[0].astype(BF16), unit_ref.shape)


def nt(left, right):
    return lax.dot_general(left, right, (((1,), (1,)), ((), ())), preferred_element_type=F32)


def turned(ring_ref, flip):
    part = ring_ref.shape[1] // NY
    begin = lax.axis_index("y") * part // LANES * LANES
    rest = pl.multiple_of(lax.axis_index("y") * part - begin, TILE)
    flip[...] = ring_ref[:, pl.ds(pl.multiple_of(begin, LANES), 2 * LANES)].T
    return flip[pl.ds(rest, part)]


def split_rows(sums, axis, keep_ref, give_ref):
    rows = keep_ref.shape[0]
    here = lax.axis_index(axis)
    keep_ref[...] = sums[pl.ds(pl.multiple_of(here * rows, TILE), rows)]
    give_ref[...] = sums[pl.ds(pl.multiple_of((1 - here) * rows, TILE), rows)].astype(BF16)


def teacher_kernel(ring_ref, keep_ref, give_ref, flip, upper):
    y = lax.axis_index("y")
    count = ring_ref.shape[1] // LANES
    for i, block in ((0, y), (1, jnp.minimum(count - y, count - 1))):
        begin = pl.multiple_of(block * LANES, LANES)
        flip[i * LANES : (i + 1) * LANES] = ring_ref[:, pl.ds(begin, LANES)].T
    for k in range(count):
        first = k < count - y
        row_block = jnp.where(first, y, count - y)
        col_block = jnp.where(first, y + k, k)
        used = jnp.logical_or(first, 2 * y < count)
        col_block = jnp.where(used, col_block, 0)
        weight = jnp.where(used, jnp.where(row_block == col_block, 1.0, 2.0**0.5), 0.0)
        left = flip[pl.ds(pl.multiple_of(jnp.where(first, 0, LANES), LANES), LANES)]
        right = ring_ref[:, pl.ds(pl.multiple_of(col_block * LANES, LANES), LANES)]
        block = jnp.dot(left, right, preferred_element_type=F32)
        upper[k * LANES : (k + 1) * LANES] = weight * block
    split_rows(upper, "z1", keep_ref, give_ref)


def student_kernel(ring_s, ring_t, give_ref, flip):
    width = ring_s.shape[1]
    quad, rows = give_ref.shape[:2]
    part = quad * rows
    left = turned(ring_s, flip)
    ss = jnp.dot(left, ring_s[...], preferred_element_type=F32)
    row = lax.broadcasted_iota(jnp.int32, (part, width), 0) + lax.axis_index("y") * part
    on = row == lax.broadcasted_iota(jnp.int32, (part, width), 1)
    ss = ss - jnp.where(on, ring_s.shape[0] / width, 0.0)
    st = -jnp.dot(left, ring_t[...], preferred_element_type=F32)
    for at, sums in ((0, ss), (width, st)):
        for i in range(quad):
            give_ref[i, :, at : at + width] = sums[i * rows : (i + 1) * rows].astype(BF16)


def quad_kernel(got_ref, total_ref, send_ref):
    total = jnp.sum(got_ref[...].astype(F32), axis=0)
    total_ref[...] = total
    send_ref[...] = total.astype(BF16)


def halve_kernel(mine_ref, got_ref, keep_ref, give_ref, sums):
    sums[...] = mine_ref[...] + got_ref[...].astype(F32)
    split_rows(sums, "z2", keep_ref, give_ref)


def energy_kernel(mine_ref, got_ref, e_ref):
    tt = mine_ref[...] + got_ref[...].astype(F32)
    e_ref[...] = jnp.broadcast_to(jnp.sum(tt * tt, axis=0, keepdims=True), e_ref.shape)


def energies_kernel(e_ref, out_ref):
    out_ref[...] = jnp.broadcast_to(jnp.sum(e_ref[...], axis=0), out_ref.shape)


def add_kernel(mine_ref, got_ref, total_ref, send_ref):
    total = mine_ref[...] + got_ref[...].astype(F32)
    total_ref[...] = total
    send_ref[...] = total.astype(BF16)


def exchange_kernel(mine_ref, got_ref, out_ref):
    out_ref[...] = jnp.broadcast_to(
        (mine_ref[...] + got_ref[...].astype(F32)).astype(BF16), out_ref.shape
    )


def pull_kernel(whole, ring_s, ring_t, e_ref, f_ref, out_ref):
    part, width = whole.shape[0], whole.shape[1] // 2
    pull = nt(whole[:, :width], ring_s[...]) + nt(whole[:, width:], ring_t[...])
    parts = split3(e_ref[0:1] + f_ref[0:1])
    n = out_ref.shape[2]
    for i in range(NY):
        out_ref[i, 0:part] = pull[:, i * n : (i + 1) * n].astype(BF16)
        out_ref[i, part:] = parts


def finish_kernel(scale, diag, blocks_ref, student_ref, out_ref):
    n, width = student_ref.shape
    part = width // NY
    parts = sum(join3(blocks_ref[i, part:]) for i in range(NY))
    energy = jnp.sum(parts, axis=1, keepdims=True)
    factor = scale / energy
    unit_f, norm_s = unit_rows(student_ref[...])
    pull_t = jnp.concatenate([blocks_ref[i, 0:part].astype(F32) for i in range(NY)], axis=0)
    pull = (pull_t.T + diag * unit_f.astype(BF16).astype(F32)) * factor
    along = jnp.sum(pull * unit_f, axis=-1, keepdims=True)
    out_ref[...] = (pull - along * unit_f) / norm_s


def swap(x, axis):
    return lax.ppermute(x, axis, [(0, 1), (1, 0)])


def gather_y(x):
    n, width = x.shape
    (copies,) = call(units_kernel, [struct((NY, n, width), BF16)], [x], 5 * n * width)
    return lax.all_to_all(copies, "y", 0, 0).reshape(NY * n, width)


def on_device(student, teacher):
    n, width = student.shape
    batch_texts = n * lax.axis_size(COL)
    total_texts = n * lax.axis_size(ALL)
    part = width // NY
    rows = part // 4
    texts = n * NY
    mac = texts * part * width

    def pair(rows, wide):
        return [struct((rows, wide), F32), struct((rows, wide), BF16)]

    ring_t = gather_y(teacher)
    ring_s = gather_y(student)

    quad = ("z2", "z1")
    tt, tt_give = call(
        teacher_kernel,
        pair(width // 2, LANES),
        [ring_t],
        mac,
        [pltpu.VMEM((2 * LANES, texts), BF16), pltpu.VMEM((width, LANES), F32)],
    )
    tt_got = swap(tt_give, "z1")
    tt, tt_give = call(
        halve_kernel,
        pair(width // 4, LANES),
        [tt, tt_got],
        part * width,
        [pltpu.VMEM((width // 2, LANES), F32)],
    )
    tt_got = swap(tt_give, "z2")
    tt, tt_give = call(add_kernel, pair(width // 4, LANES), [tt, tt_got], rows * width)
    (give,) = call(
        student_kernel,
        [struct((4, rows, 2 * width), BF16)],
        [ring_s, ring_t],
        4 * mac,
        [pltpu.VMEM((2 * LANES, texts), BF16)],
    )
    give = lax.optimization_barrier((give, tt_give))[0]
    tt_got = swap(tt_give, "zf")
    got = lax.all_to_all(give, quad, 0, 0)
    keep, give = call(
        quad_kernel, pair(rows, 2 * width), [got], 4 * rows * width, after=[tt_got]
    )
    got = swap(give, "zf")
    some = ("xc", "z2", "z1")
    (e,) = call(
        energy_kernel,
        [struct((lax.axis_size(some), 1, LANES), F32)],
        [tt, tt_got],
        3 * rows * width,
        after=[give],
    )
    e = lax.all_to_all(e, some, 0, 0)
    (mine,) = call(
        exchange_kernel,
        [struct((4, rows, 2 * width), BF16)],
        [keep, got],
        2 * rows * width,
        after=[e],
    )
    whole = lax.all_to_all(mine, quad, 0, 0).reshape(part, 2 * width)
    (e,) = call(energies_kernel, [struct((8, LANES), F32)], [e], e.size, after=[mine])
    e_far = swap(e, "zh")
    (blocks,) = call(
        pull_kernel,
        [struct((NY, part + TILE, n), BF16)],
        [whole, ring_s, ring_t, e, e_far],
        4 * mac,
    )
    blocks = lax.all_to_all(blocks, "y", 0, 0)
    (out,) = call(
        functools.partial(finish_kernel, batch_texts**0.5 * total_texts, batch_texts / width),
        [struct((n, width), F32)],
        [blocks, student],
        12 * n * width,
    )
    return out


def solution(mesh):
    rows, cols = mesh.devices.shape
    fine = Mesh(mesh.devices.reshape(2, rows // 2, 2, 2, 2, cols // NZ), ALL)
    return jax.shard_map(
        on_device,
        mesh=fine,
        in_specs=(P(ALL, None), P(ALL, None)),
        out_specs=P(ALL, None),
        check_vma=False,
    )
```

```python
import functools

import jax
import jax.numpy as jnp
from jax import lax
from jax.experimental import pallas as pl
from jax.experimental.pallas import tpu as pltpu
from jax.sharding import Mesh, PartitionSpec as P

NY = 4
NZ = 8
LANES = 128
TILE = 16
F32 = jnp.float32
BF16 = jnp.bfloat16
COL = ("zf", "z2", "z1", "y")
ALL = ("zh", "xc") + COL
VMEM_LIMIT = 12 * 1024 * 1024


def call(body, out_shape, operands, flops, scratch=(), after=()):
    size = sum(a.size * a.dtype.itemsize for a in operands)
    size += sum(s.size * s.dtype.itemsize for s in out_shape)
    count, extra = len(operands), len(after)

    def run(*refs):
        body(*refs[:count], *refs[count + extra :])

    whole = pl.BlockSpec(memory_space=pltpu.VMEM)
    return pl.pallas_call(
        run,
        out_shape=out_shape,
        in_specs=[whole] * count + [pl.BlockSpec(memory_space=pl.ANY)] * extra,
        out_specs=[whole] * len(out_shape),
        scratch_shapes=scratch,
        compiler_params=pltpu.CompilerParams(vmem_limit_bytes=VMEM_LIMIT),
        cost_estimate=pl.CostEstimate(flops=flops, bytes_accessed=size, transcendentals=0),
    )(*operands, *after)


def struct(shape, dtype):
    return jax.ShapeDtypeStruct(shape, dtype)


def unit_rows(values):
    wide = values.astype(F32)
    length = jnp.sqrt(jnp.sum(wide * wide, axis=-1, keepdims=True) + 1e-06)
    return (wide / length, length)


def split3(e):
    high = e.astype(BF16).astype(F32)
    mid = (e - high).astype(BF16).astype(F32)
    low = e - high - mid
    row = lax.broadcasted_iota(jnp.int32, (TILE, LANES), 0)
    parts = jnp.where(row == 0, high, jnp.where(row == 1, mid, jnp.where(row == 2, low, 0.0)))
    return parts.astype(BF16)


def join3(parts):
    return jnp.sum(parts.astype(F32), axis=0, keepdims=True)


def units_kernel(x_ref, unit_ref):
    unit_ref[...] = jnp.broadcast_to(unit_rows(x_ref[...])[0].astype(BF16), unit_ref.shape)


def nt(left, right):
    return lax.dot_general(left, right, (((1,), (1,)), ((), ())), preferred_element_type=F32)


def turned(ring_ref, flip):
    part = ring_ref.shape[1] // NY
    begin = lax.axis_index("y") * part // LANES * LANES
    rest = pl.multiple_of(lax.axis_index("y") * part - begin, TILE)
    flip[...] = ring_ref[:, pl.ds(pl.multiple_of(begin, LANES), 2 * LANES)].T
    return flip[pl.ds(rest, part)]


def teacher_kernel(ring_ref, keep_ref, give1_ref, give2_ref, give3_ref, flip, upper):
    y = lax.axis_index("y")
    count = ring_ref.shape[1] // LANES
    for i, block in ((0, y), (1, jnp.minimum(count - y, count - 1))):
        begin = pl.multiple_of(block * LANES, LANES)
        flip[i * LANES : (i + 1) * LANES] = ring_ref[:, pl.ds(begin, LANES)].T
    for k in range(count):
        first = k < count - y
        row_block = jnp.where(first, y, count - y)
        col_block = jnp.where(first, y + k, k)
        used = jnp.logical_or(first, 2 * y < count)
        col_block = jnp.where(used, col_block, 0)
        weight = jnp.where(used, jnp.where(row_block == col_block, 1.0, 2.0**0.5), 0.0)
        left = flip[pl.ds(pl.multiple_of(jnp.where(first, 0, LANES), LANES), LANES)]
        right = ring_ref[:, pl.ds(pl.multiple_of(col_block * LANES, LANES), LANES)]
        block = jnp.dot(left, right, preferred_element_type=F32)
        upper[k * LANES : (k + 1) * LANES] = weight * block
    z1, z2 = lax.axis_index("z1"), lax.axis_index("z2")
    rows = keep_ref.shape[0]
    for m, ref in enumerate((keep_ref, give1_ref, give2_ref, give3_ref)):
        piece = 2 * (1 - z2 if m & 2 else z2) + (1 - z1 if m & 1 else z1)
        ref[...] = upper[pl.ds(pl.multiple_of(piece * rows, TILE), rows)].astype(ref.dtype)


def student_kernel(ring_s, ring_t, give_ref, flip):
    width = ring_s.shape[1]
    quad, rows = give_ref.shape[:2]
    part = quad * rows
    left = turned(ring_s, flip)
    ss = jnp.dot(left, ring_s[...], preferred_element_type=F32)
    row = lax.broadcasted_iota(jnp.int32, (part, width), 0) + lax.axis_index("y") * part
    on = row == lax.broadcasted_iota(jnp.int32, (part, width), 1)
    ss = ss - jnp.where(on, ring_s.shape[0] / width, 0.0)
    st = -jnp.dot(left, ring_t[...], preferred_element_type=F32)
    for at, sums in ((0, ss), (width, st)):
        for i in range(quad):
            give_ref[i, :, at : at + width] = sums[i * rows : (i + 1) * rows].astype(BF16)


def quad_kernel(got_ref, total_ref, send_ref):
    total = jnp.sum(got_ref[...].astype(F32), axis=0)
    total_ref[...] = total
    send_ref[...] = total.astype(BF16)


def energy_kernel(mine_ref, got_ref, e_ref):
    tt = mine_ref[...] + got_ref[...].astype(F32)
    e_ref[...] = jnp.broadcast_to(jnp.sum(tt * tt, axis=0, keepdims=True), e_ref.shape)


def energies_kernel(e_ref, out_ref):
    out_ref[...] = jnp.broadcast_to(jnp.sum(e_ref[...], axis=0), out_ref.shape)


def add_kernel(mine_ref, got1_ref, got2_ref, got3_ref, total_ref, send_ref):
    total = mine_ref[...]
    for ref in (got1_ref, got2_ref, got3_ref):
        total = total + ref[...].astype(F32)
    total_ref[...] = total
    send_ref[...] = total.astype(BF16)


def exchange_kernel(mine_ref, got_ref, out_ref):
    out_ref[...] = jnp.broadcast_to(
        (mine_ref[...] + got_ref[...].astype(F32)).astype(BF16), out_ref.shape
    )


def pull_kernel(whole, ring_s, ring_t, e_ref, f_ref, out_ref):
    part, width = whole.shape[0], whole.shape[1] // 2
    pull = nt(whole[:, :width], ring_s[...]) + nt(whole[:, width:], ring_t[...])
    parts = split3(e_ref[0:1] + f_ref[0:1])
    n = out_ref.shape[2]
    for i in range(NY):
        out_ref[i, 0:part] = pull[:, i * n : (i + 1) * n].astype(BF16)
        out_ref[i, part:] = parts


def finish_kernel(scale, diag, blocks_ref, student_ref, out_ref):
    n, width = student_ref.shape
    part = width // NY
    parts = sum(join3(blocks_ref[i, part:]) for i in range(NY))
    energy = jnp.sum(parts, axis=1, keepdims=True)
    factor = scale / energy
    unit_f, norm_s = unit_rows(student_ref[...])
    pull_t = jnp.concatenate([blocks_ref[i, 0:part].astype(F32) for i in range(NY)], axis=0)
    pull = (pull_t.T + diag * unit_f.astype(BF16).astype(F32)) * factor
    along = jnp.sum(pull * unit_f, axis=-1, keepdims=True)
    out_ref[...] = (pull - along * unit_f) / norm_s


def swap(x, axis):
    return lax.ppermute(x, axis, [(0, 1), (1, 0)])


def gather_y(x):
    n, width = x.shape
    block = n // 2
    copies = pl.pallas_call(
        units_kernel,
        out_shape=struct((NY, n, width), BF16),
        grid=(n // block,),
        in_specs=[pl.BlockSpec((block, width), lambda i: (i, 0))],
        out_specs=pl.BlockSpec((NY, block, width), lambda i: (0, i, 0)),
        compiler_params=pltpu.CompilerParams(vmem_limit_bytes=VMEM_LIMIT),
        cost_estimate=pl.CostEstimate(
            flops=5 * n * width, bytes_accessed=10 * n * width, transcendentals=0
        ),
    )(x)
    return lax.all_to_all(copies, "y", 0, 0).reshape(NY * n, width)


def on_device(student, teacher):
    n, width = student.shape
    batch_texts = n * lax.axis_size(COL)
    total_texts = n * lax.axis_size(ALL)
    part = width // NY
    rows = part // 4
    texts = n * NY
    mac = texts * part * width

    def pair(rows, wide):
        return [struct((rows, wide), F32), struct((rows, wide), BF16)]

    ring_t = gather_y(teacher)
    ring_s = gather_y(student)

    quad = ("z2", "z1")
    piece = width // 4
    tt, *tt_give = call(
        teacher_kernel,
        [struct((piece, LANES), F32)] + [struct((piece, LANES), BF16)] * 3,
        [ring_t],
        mac,
        [pltpu.VMEM((2 * LANES, texts), BF16), pltpu.VMEM((width, LANES), F32)],
    )
    tt_got = [
        lax.ppermute(x, quad, [(i, i ^ m) for i in range(4)]) for m, x in zip((1, 2, 3), tt_give)
    ]
    tt, tt_give = call(add_kernel, pair(piece, LANES), [tt, *tt_got], 3 * piece * LANES)
    (give,) = call(
        student_kernel,
        [struct((4, rows, 2 * width), BF16)],
        [ring_s, ring_t],
        4 * mac,
        [pltpu.VMEM((2 * LANES, texts), BF16)],
    )
    give = lax.optimization_barrier((give, tt_give))[0]
    tt_got = swap(tt_give, "zf")
    got = lax.all_to_all(give, quad, 0, 0)
    keep, give = call(
        quad_kernel, pair(rows, 2 * width), [got], 4 * rows * width, after=[tt_got]
    )
    got = swap(give, "zf")
    some = ("xc", "z2", "z1")
    (e,) = call(
        energy_kernel,
        [struct((lax.axis_size(some), 1, LANES), F32)],
        [tt, tt_got],
        3 * rows * width,
        after=[give],
    )
    e = lax.all_to_all(e, some, 0, 0)
    (mine,) = call(
        exchange_kernel,
        [struct((4, rows, 2 * width), BF16)],
        [keep, got],
        2 * rows * width,
        after=[e],
    )
    whole = lax.all_to_all(mine, quad, 0, 0).reshape(part, 2 * width)
    (e,) = call(energies_kernel, [struct((8, LANES), F32)], [e], e.size, after=[mine])
    e_far = swap(e, "zh")
    (blocks,) = call(
        pull_kernel,
        [struct((NY, part + TILE, n), BF16)],
        [whole, ring_s, ring_t, e, e_far],
        4 * mac,
    )
    blocks = lax.all_to_all(blocks, "y", 0, 0)
    (out,) = call(
        functools.partial(finish_kernel, batch_texts**0.5 * total_texts, batch_texts / width),
        [struct((n, width), F32)],
        [blocks, student],
        12 * n * width,
    )
    return out


def solution(mesh):
    rows, cols = mesh.devices.shape
    fine = Mesh(mesh.devices.reshape(2, rows // 2, 2, 2, 2, cols // NZ), ALL)
    return jax.shard_map(
        on_device,
        mesh=fine,
        in_specs=(P(ALL, None), P(ALL, None)),
        out_specs=P(ALL, None),
        check_vma=False,
    )
```

```python
import functools

import jax
import jax.numpy as jnp
from jax import lax
from jax.experimental import pallas as pl
from jax.experimental.pallas import tpu as pltpu
from jax.sharding import Mesh, PartitionSpec as P

NY = 4
NZ = 8
LANES = 128
TILE = 16
F32 = jnp.float32
BF16 = jnp.bfloat16
COL = ("zf", "z2", "z1", "y")
ALL = ("zh", "xc") + COL
VMEM_LIMIT = 12 * 1024 * 1024


def call(body, out_shape, operands, flops, scratch=(), after=()):
    size = sum(a.size * a.dtype.itemsize for a in operands)
    size += sum(s.size * s.dtype.itemsize for s in out_shape)
    count, extra = len(operands), len(after)

    def run(*refs):
        body(*refs[:count], *refs[count + extra :])

    whole = pl.BlockSpec(memory_space=pltpu.VMEM)
    return pl.pallas_call(
        run,
        out_shape=out_shape,
        in_specs=[whole] * count + [pl.BlockSpec(memory_space=pl.ANY)] * extra,
        out_specs=[whole] * len(out_shape),
        scratch_shapes=scratch,
        compiler_params=pltpu.CompilerParams(vmem_limit_bytes=VMEM_LIMIT),
        cost_estimate=pl.CostEstimate(flops=flops, bytes_accessed=size, transcendentals=0),
    )(*operands, *after)


def struct(shape, dtype):
    return jax.ShapeDtypeStruct(shape, dtype)


def unit_rows(values):
    wide = values.astype(F32)
    length = jnp.sqrt(jnp.sum(wide * wide, axis=-1, keepdims=True) + 1e-06)
    return (wide / length, length)


def split3(e):
    high = e.astype(BF16).astype(F32)
    mid = (e - high).astype(BF16).astype(F32)
    low = e - high - mid
    row = lax.broadcasted_iota(jnp.int32, (TILE, LANES), 0)
    parts = jnp.where(row == 0, high, jnp.where(row == 1, mid, jnp.where(row == 2, low, 0.0)))
    return parts.astype(BF16)


def join3(parts):
    return jnp.sum(parts.astype(F32), axis=0, keepdims=True)


def send_copies(src, out_ref, sems):
    copies = [pltpu.make_async_copy(src, out_ref.at[i], sems.at[i]) for i in range(out_ref.shape[0])]
    for copy in copies:
        copy.start()
    for copy in copies:
        copy.wait()


def units_kernel(x_ref, out_ref, x_here, unit, in_sem, out_sems):
    load = pltpu.make_async_copy(x_ref, x_here, in_sem)
    load.start()
    load.wait()
    unit[...] = unit_rows(x_here[...])[0].astype(BF16)
    send_copies(unit, out_ref, out_sems)


def nt(left, right):
    return lax.dot_general(left, right, (((1,), (1,)), ((), ())), preferred_element_type=F32)


def turned(ring_ref, flip):
    part = ring_ref.shape[1] // NY
    begin = lax.axis_index("y") * part // LANES * LANES
    rest = pl.multiple_of(lax.axis_index("y") * part - begin, TILE)
    flip[...] = ring_ref[:, pl.ds(pl.multiple_of(begin, LANES), 2 * LANES)].T
    return flip[pl.ds(rest, part)]


def split_rows(sums, axis, keep_ref, give_ref):
    rows = keep_ref.shape[0]
    here = lax.axis_index(axis)
    keep_ref[...] = sums[pl.ds(pl.multiple_of(here * rows, TILE), rows)]
    give_ref[...] = sums[pl.ds(pl.multiple_of((1 - here) * rows, TILE), rows)].astype(BF16)


def teacher_kernel(ring_ref, keep_ref, give_ref, flip, upper):
    y = lax.axis_index("y")
    count = ring_ref.shape[1] // LANES
    for i, block in ((0, y), (1, jnp.minimum(count - y, count - 1))):
        begin = pl.multiple_of(block * LANES, LANES)
        flip[i * LANES : (i + 1) * LANES] = ring_ref[:, pl.ds(begin, LANES)].T
    for k in range(count):
        first = k < count - y
        row_block = jnp.where(first, y, count - y)
        col_block = jnp.where(first, y + k, k)
        used = jnp.logical_or(first, 2 * y < count)
        col_block = jnp.where(used, col_block, 0)
        weight = jnp.where(used, jnp.where(row_block == col_block, 1.0, 2.0**0.5), 0.0)
        left = flip[pl.ds(pl.multiple_of(jnp.where(first, 0, LANES), LANES), LANES)]
        right = ring_ref[:, pl.ds(pl.multiple_of(col_block * LANES, LANES), LANES)]
        block = jnp.dot(left, right, preferred_element_type=F32)
        upper[k * LANES : (k + 1) * LANES] = weight * block
    split_rows(upper, "z1", keep_ref, give_ref)


def student_kernel(ring_s, ring_t, give_ref, flip):
    width = ring_s.shape[1]
    quad, rows = give_ref.shape[:2]
    part = quad * rows
    left = turned(ring_s, flip)
    ss = jnp.dot(left, ring_s[...], preferred_element_type=F32)
    row = lax.broadcasted_iota(jnp.int32, (part, width), 0) + lax.axis_index("y") * part
    on = row == lax.broadcasted_iota(jnp.int32, (part, width), 1)
    ss = ss - jnp.where(on, ring_s.shape[0] / width, 0.0)
    st = -jnp.dot(left, ring_t[...], preferred_element_type=F32)
    for at, sums in ((0, ss), (width, st)):
        for i in range(quad):
            give_ref[i, :, at : at + width] = sums[i * rows : (i + 1) * rows].astype(BF16)


def quad_kernel(got_ref, total_ref, send_ref):
    total = jnp.sum(got_ref[...].astype(F32), axis=0)
    total_ref[...] = total
    send_ref[...] = total.astype(BF16)


def halve_kernel(mine_ref, got_ref, keep_ref, give_ref, sums):
    sums[...] = mine_ref[...] + got_ref[...].astype(F32)
    split_rows(sums, "z2", keep_ref, give_ref)


def energy_kernel(mine_ref, got_ref, e_ref):
    tt = mine_ref[...] + got_ref[...].astype(F32)
    e_ref[...] = jnp.broadcast_to(jnp.sum(tt * tt, axis=0, keepdims=True), e_ref.shape)


def energies_kernel(e_ref, out_ref):
    out_ref[...] = jnp.broadcast_to(jnp.sum(e_ref[...], axis=0), out_ref.shape)


def add_kernel(mine_ref, got_ref, total_ref, send_ref):
    total = mine_ref[...] + got_ref[...].astype(F32)
    total_ref[...] = total
    send_ref[...] = total.astype(BF16)


def exchange_kernel(mine_ref, got_ref, e_ref, out_ref, total, sems):
    total[...] = (mine_ref[...] + got_ref[...].astype(F32)).astype(BF16)
    send_copies(total, out_ref, sems)


def pull_kernel(whole, ring_s, ring_t, e_ref, f_ref, out_ref):
    part, width = whole.shape[0], whole.shape[1] // 2
    pull = nt(whole[:, :width], ring_s[...]) + nt(whole[:, width:], ring_t[...])
    parts = split3(e_ref[0:1] + f_ref[0:1])
    n = out_ref.shape[2]
    for i in range(NY):
        out_ref[i, 0:part] = pull[:, i * n : (i + 1) * n].astype(BF16)
        out_ref[i, part:] = parts


def finish_kernel(scale, diag, blocks_ref, student_ref, out_ref):
    n, width = student_ref.shape
    part = width // NY
    parts = sum(join3(blocks_ref[i, part:]) for i in range(NY))
    energy = jnp.sum(parts, axis=1, keepdims=True)
    factor = scale / energy
    unit_f, norm_s = unit_rows(student_ref[...])
    pull_t = jnp.concatenate([blocks_ref[i, 0:part].astype(F32) for i in range(NY)], axis=0)
    pull = (pull_t.T + diag * unit_f.astype(BF16).astype(F32)) * factor
    along = jnp.sum(pull * unit_f, axis=-1, keepdims=True)
    out_ref[...] = (pull - along * unit_f) / norm_s


def swap(x, axis):
    return lax.ppermute(x, axis, [(0, 1), (1, 0)])


def gather_y(x):
    n, width = x.shape
    copies = pl.pallas_call(
        units_kernel,
        out_shape=struct((NY, n, width), BF16),
        in_specs=[pl.BlockSpec(memory_space=pl.ANY)],
        out_specs=pl.BlockSpec(memory_space=pl.ANY),
        scratch_shapes=[
            pltpu.VMEM((n, width), BF16),
            pltpu.VMEM((n, width), BF16),
            pltpu.SemaphoreType.DMA,
            pltpu.SemaphoreType.DMA((NY,)),
        ],
        compiler_params=pltpu.CompilerParams(vmem_limit_bytes=VMEM_LIMIT),
        cost_estimate=pl.CostEstimate(
            flops=5 * n * width, bytes_accessed=10 * n * width, transcendentals=0
        ),
    )(x)
    return lax.all_to_all(copies, "y", 0, 0).reshape(NY * n, width)


def on_device(student, teacher):
    n, width = student.shape
    batch_texts = n * lax.axis_size(COL)
    total_texts = n * lax.axis_size(ALL)
    part = width // NY
    rows = part // 4
    texts = n * NY
    mac = texts * part * width

    def pair(rows, wide):
        return [struct((rows, wide), F32), struct((rows, wide), BF16)]

    ring_t = gather_y(teacher)
    ring_s = gather_y(student)

    quad = ("z2", "z1")
    tt, tt_give = call(
        teacher_kernel,
        pair(width // 2, LANES),
        [ring_t],
        mac,
        [pltpu.VMEM((2 * LANES, texts), BF16), pltpu.VMEM((width, LANES), F32)],
    )
    tt_got = swap(tt_give, "z1")
    tt, tt_give = call(
        halve_kernel,
        pair(width // 4, LANES),
        [tt, tt_got],
        part * width,
        [pltpu.VMEM((width // 2, LANES), F32)],
    )
    tt_got = swap(tt_give, "z2")
    tt, tt_give = call(add_kernel, pair(width // 4, LANES), [tt, tt_got], rows * width)
    (give,) = call(
        student_kernel,
        [struct((4, rows, 2 * width), BF16)],
        [ring_s, ring_t],
        4 * mac,
        [pltpu.VMEM((2 * LANES, texts), BF16)],
    )
    give = lax.optimization_barrier((give, tt_give))[0]
    tt_got = swap(tt_give, "zf")
    got = lax.all_to_all(give, quad, 0, 0)
    keep, give = call(
        quad_kernel, pair(rows, 2 * width), [got], 4 * rows * width, after=[tt_got]
    )
    got = swap(give, "zf")
    some = ("xc", "z2", "z1")
    (e,) = call(
        energy_kernel,
        [struct((lax.axis_size(some), 1, LANES), F32)],
        [tt, tt_got],
        3 * rows * width,
        after=[give],
    )
    e = lax.all_to_all(e, some, 0, 0)
    vmem, anywhere = pl.BlockSpec(memory_space=pltpu.VMEM), pl.BlockSpec(memory_space=pl.ANY)
    mine = pl.pallas_call(
        exchange_kernel,
        out_shape=struct((4, rows, 2 * width), BF16),
        in_specs=[vmem, vmem, anywhere],
        out_specs=anywhere,
        scratch_shapes=[pltpu.VMEM((rows, 2 * width), BF16), pltpu.SemaphoreType.DMA((4,))],
        compiler_params=pltpu.CompilerParams(vmem_limit_bytes=VMEM_LIMIT),
        cost_estimate=pl.CostEstimate(
            flops=2 * rows * width, bytes_accessed=28 * rows * width, transcendentals=0
        ),
    )(keep, got, e)
    whole = lax.all_to_all(mine, quad, 0, 0).reshape(part, 2 * width)
    (e,) = call(energies_kernel, [struct((8, LANES), F32)], [e], e.size, after=[mine])
    e_far = swap(e, "zh")
    (blocks,) = call(
        pull_kernel,
        [struct((NY, part + TILE, n), BF16)],
        [whole, ring_s, ring_t, e, e_far],
        4 * mac,
    )
    blocks = lax.all_to_all(blocks, "y", 0, 0)
    (out,) = call(
        functools.partial(finish_kernel, batch_texts**0.5 * total_texts, batch_texts / width),
        [struct((n, width), F32)],
        [blocks, student],
        12 * n * width,
    )
    return out


def solution(mesh):
    rows, cols = mesh.devices.shape
    fine = Mesh(mesh.devices.reshape(2, rows // 2, 2, 2, 2, cols // NZ), ALL)
    return jax.shard_map(
        on_device,
        mesh=fine,
        in_specs=(P(ALL, None), P(ALL, None)),
        out_specs=P(ALL, None),
        check_vma=False,
    )
```

```python
import functools

import jax
import jax.numpy as jnp
from jax import lax
from jax.experimental import pallas as pl
from jax.experimental.pallas import tpu as pltpu
from jax.sharding import Mesh, PartitionSpec as P

NY = 4
NZ = 8
LANES = 128
TILE = 16
F32 = jnp.float32
BF16 = jnp.bfloat16
COL = ("zf", "z2", "z1", "y")
ALL = ("zh", "xc") + COL
VMEM_LIMIT = 12 * 1024 * 1024


def call(body, out_shape, operands, flops, scratch=(), after=()):
    size = sum(a.size * a.dtype.itemsize for a in operands)
    size += sum(s.size * s.dtype.itemsize for s in out_shape)
    count, extra = len(operands), len(after)

    def run(*refs):
        body(*refs[:count], *refs[count + extra :])

    whole = pl.BlockSpec(memory_space=pltpu.VMEM)
    return pl.pallas_call(
        run,
        out_shape=out_shape,
        in_specs=[whole] * count + [pl.BlockSpec(memory_space=pl.ANY)] * extra,
        out_specs=[whole] * len(out_shape),
        scratch_shapes=scratch,
        compiler_params=pltpu.CompilerParams(vmem_limit_bytes=VMEM_LIMIT),
        cost_estimate=pl.CostEstimate(flops=flops, bytes_accessed=size, transcendentals=0),
    )(*operands, *after)


def struct(shape, dtype):
    return jax.ShapeDtypeStruct(shape, dtype)


def unit_rows(values):
    wide = values.astype(F32)
    length = jnp.sqrt(jnp.sum(wide * wide, axis=-1, keepdims=True) + 1e-06)
    return (wide / length, length)


def split3(e):
    high = e.astype(BF16).astype(F32)
    mid = (e - high).astype(BF16).astype(F32)
    low = e - high - mid
    row = lax.broadcasted_iota(jnp.int32, (TILE, LANES), 0)
    parts = jnp.where(row == 0, high, jnp.where(row == 1, mid, jnp.where(row == 2, low, 0.0)))
    return parts.astype(BF16)


def join3(parts):
    return jnp.sum(parts.astype(F32), axis=0, keepdims=True)


def send_copies(src, out_ref, sems):
    copies = [pltpu.make_async_copy(src, out_ref.at[i], sems.at[i]) for i in range(out_ref.shape[0])]
    for copy in copies:
        copy.start()
    for copy in copies:
        copy.wait()


def units_kernel(x_ref, out_ref, x_here, unit, in_sem, out_sems):
    load = pltpu.make_async_copy(x_ref, x_here, in_sem)
    load.start()
    load.wait()
    unit[...] = unit_rows(x_here[...])[0].astype(BF16)
    send_copies(unit, out_ref, out_sems)


def nt(left, right):
    return lax.dot_general(left, right, (((1,), (1,)), ((), ())), preferred_element_type=F32)


def turned(ring_ref, flip):
    part = ring_ref.shape[1] // NY
    begin = lax.axis_index("y") * part // LANES * LANES
    rest = pl.multiple_of(lax.axis_index("y") * part - begin, TILE)
    flip[...] = ring_ref[:, pl.ds(pl.multiple_of(begin, LANES), 2 * LANES)].T
    return flip[pl.ds(rest, part)]


def split_rows(sums, axis, keep_ref, give_ref):
    rows = keep_ref.shape[0]
    here = lax.axis_index(axis)
    keep_ref[...] = sums[pl.ds(pl.multiple_of(here * rows, TILE), rows)]
    give_ref[...] = sums[pl.ds(pl.multiple_of((1 - here) * rows, TILE), rows)].astype(BF16)


def teacher_kernel(ring_ref, keep_ref, give_ref, flip, upper):
    y = lax.axis_index("y")
    count = ring_ref.shape[1] // LANES
    for i, block in ((0, y), (1, jnp.minimum(count - y, count - 1))):
        begin = pl.multiple_of(block * LANES, LANES)
        flip[i * LANES : (i + 1) * LANES] = ring_ref[:, pl.ds(begin, LANES)].T
    for k in range(count):
        first = k < count - y
        row_block = jnp.where(first, y, count - y)
        col_block = jnp.where(first, y + k, k)
        used = jnp.logical_or(first, 2 * y < count)
        col_block = jnp.where(used, col_block, 0)
        weight = jnp.where(used, jnp.where(row_block == col_block, 1.0, 2.0**0.5), 0.0)
        left = flip[pl.ds(pl.multiple_of(jnp.where(first, 0, LANES), LANES), LANES)]
        right = ring_ref[:, pl.ds(pl.multiple_of(col_block * LANES, LANES), LANES)]
        block = jnp.dot(left, right, preferred_element_type=F32)
        upper[k * LANES : (k + 1) * LANES] = weight * block
    split_rows(upper, "z1", keep_ref, give_ref)


def student_kernel(ring_s, ring_t, give_ref, flip):
    width = ring_s.shape[1]
    quad, rows = give_ref.shape[:2]
    part = quad * rows
    left = turned(ring_s, flip)
    ss = jnp.dot(left, ring_s[...], preferred_element_type=F32)
    row = lax.broadcasted_iota(jnp.int32, (part, width), 0) + lax.axis_index("y") * part
    on = row == lax.broadcasted_iota(jnp.int32, (part, width), 1)
    ss = ss - jnp.where(on, ring_s.shape[0] / width, 0.0)
    st = -jnp.dot(left, ring_t[...], preferred_element_type=F32)
    for at, sums in ((0, ss), (width, st)):
        for i in range(quad):
            give_ref[i, :, at : at + width] = sums[i * rows : (i + 1) * rows].astype(BF16)


def quad_kernel(got_ref, total_ref, send_ref):
    total = jnp.sum(got_ref[...].astype(F32), axis=0)
    total_ref[...] = total
    send_ref[...] = total.astype(BF16)


def halve_kernel(mine_ref, got_ref, keep_ref, give_ref, sums):
    sums[...] = mine_ref[...] + got_ref[...].astype(F32)
    split_rows(sums, "z2", keep_ref, give_ref)


def energy_kernel(mine_ref, got_ref, e_ref):
    tt = mine_ref[...] + got_ref[...].astype(F32)
    e_ref[...] = jnp.broadcast_to(jnp.sum(tt * tt, axis=0, keepdims=True), e_ref.shape)


def energies_kernel(e_ref, out_ref):
    out_ref[...] = jnp.broadcast_to(jnp.sum(e_ref[...], axis=0), out_ref.shape)


def add_kernel(mine_ref, got_ref, total_ref, send_ref):
    total = mine_ref[...] + got_ref[...].astype(F32)
    total_ref[...] = total
    send_ref[...] = total.astype(BF16)


def exchange_kernel(mine_ref, got_ref, out_ref):
    out_ref[...] = jnp.broadcast_to(
        (mine_ref[...] + got_ref[...].astype(F32)).astype(BF16), out_ref.shape
    )


def pull_kernel(whole, ring_s, ring_t, e_ref, f_ref, out_ref):
    part, width = whole.shape[0], whole.shape[1] // 2
    pull = nt(whole[:, :width], ring_s[...]) + nt(whole[:, width:], ring_t[...])
    parts = split3(e_ref[0:1] + f_ref[0:1])
    n = out_ref.shape[2]
    for i in range(NY):
        out_ref[i, 0:part] = pull[:, i * n : (i + 1) * n].astype(BF16)
        out_ref[i, part:] = parts


def finish_kernel(scale, diag, blocks_ref, student_ref, out_ref):
    n, width = student_ref.shape
    part = width // NY
    parts = sum(join3(blocks_ref[i, part:]) for i in range(NY))
    energy = jnp.sum(parts, axis=1, keepdims=True)
    factor = scale / energy
    unit_f, norm_s = unit_rows(student_ref[...])
    pull_t = jnp.concatenate([blocks_ref[i, 0:part].astype(F32) for i in range(NY)], axis=0)
    pull = (pull_t.T + diag * unit_f.astype(BF16).astype(F32)) * factor
    along = jnp.sum(pull * unit_f, axis=-1, keepdims=True)
    out_ref[...] = (pull - along * unit_f) / norm_s


def swap(x, axis):
    return lax.ppermute(x, axis, [(0, 1), (1, 0)])


def gather_y(x):
    n, width = x.shape
    copies = pl.pallas_call(
        units_kernel,
        out_shape=struct((NY, n, width), BF16),
        in_specs=[pl.BlockSpec(memory_space=pl.ANY)],
        out_specs=pl.BlockSpec(memory_space=pl.ANY),
        scratch_shapes=[
            pltpu.VMEM((n, width), BF16),
            pltpu.VMEM((n, width), BF16),
            pltpu.SemaphoreType.DMA,
            pltpu.SemaphoreType.DMA((NY,)),
        ],
        compiler_params=pltpu.CompilerParams(vmem_limit_bytes=60 * 1024 * 1024),
        cost_estimate=pl.CostEstimate(
            flops=5 * n * width, bytes_accessed=10 * n * width, transcendentals=0
        ),
    )(x)
    return lax.all_to_all(copies, "y", 0, 0).reshape(NY * n, width)


def on_device(student, teacher):
    n, width = student.shape
    batch_texts = n * lax.axis_size(COL)
    total_texts = n * lax.axis_size(ALL)
    part = width // NY
    rows = part // 4
    texts = n * NY
    mac = texts * part * width

    def pair(rows, wide):
        return [struct((rows, wide), F32), struct((rows, wide), BF16)]

    ring_t = gather_y(teacher)
    ring_s = gather_y(student)

    quad = ("z2", "z1")
    tt, tt_give = call(
        teacher_kernel,
        pair(width // 2, LANES),
        [ring_t],
        mac,
        [pltpu.VMEM((2 * LANES, texts), BF16), pltpu.VMEM((width, LANES), F32)],
    )
    tt_got = swap(tt_give, "z1")
    tt, tt_give = call(
        halve_kernel,
        pair(width // 4, LANES),
        [tt, tt_got],
        part * width,
        [pltpu.VMEM((width // 2, LANES), F32)],
    )
    tt_got = swap(tt_give, "z2")
    tt, tt_give = call(add_kernel, pair(width // 4, LANES), [tt, tt_got], rows * width)
    (give,) = call(
        student_kernel,
        [struct((4, rows, 2 * width), BF16)],
        [ring_s, ring_t],
        4 * mac,
        [pltpu.VMEM((2 * LANES, texts), BF16)],
    )
    give = lax.optimization_barrier((give, tt_give))[0]
    tt_got = swap(tt_give, "zf")
    got = lax.all_to_all(give, quad, 0, 0)
    keep, give = call(
        quad_kernel, pair(rows, 2 * width), [got], 4 * rows * width, after=[tt_got]
    )
    got = swap(give, "zf")
    some = ("xc", "z2", "z1")
    (e,) = call(
        energy_kernel,
        [struct((lax.axis_size(some), 1, LANES), F32)],
        [tt, tt_got],
        3 * rows * width,
        after=[give],
    )
    e = lax.all_to_all(e, some, 0, 0)
    (mine,) = call(
        exchange_kernel,
        [struct((4, rows, 2 * width), BF16)],
        [keep, got],
        2 * rows * width,
        after=[e],
    )
    whole = lax.all_to_all(mine, quad, 0, 0).reshape(part, 2 * width)
    (e,) = call(energies_kernel, [struct((8, LANES), F32)], [e], e.size, after=[mine])
    e_far = swap(e, "zh")
    (blocks,) = call(
        pull_kernel,
        [struct((NY, part + TILE, n), BF16)],
        [whole, ring_s, ring_t, e, e_far],
        4 * mac,
    )
    blocks = lax.all_to_all(blocks, "y", 0, 0)
    (out,) = call(
        functools.partial(finish_kernel, batch_texts**0.5 * total_texts, batch_texts / width),
        [struct((n, width), F32)],
        [blocks, student],
        12 * n * width,
    )
    return out


def solution(mesh):
    rows, cols = mesh.devices.shape
    fine = Mesh(mesh.devices.reshape(2, rows // 2, 2, 2, 2, cols // NZ), ALL)
    return jax.shard_map(
        on_device,
        mesh=fine,
        in_specs=(P(ALL, None), P(ALL, None)),
        out_specs=P(ALL, None),
        check_vma=False,
    )
```

```python
import functools

import jax
import jax.numpy as jnp
from jax import lax
from jax.experimental import pallas as pl
from jax.experimental.pallas import tpu as pltpu
from jax.sharding import Mesh, PartitionSpec as P

NY = 4
NZ = 8
LANES = 128
TILE = 16
F32 = jnp.float32
BF16 = jnp.bfloat16
COL = ("zf", "z2", "z1", "y")
ALL = ("zh", "xc") + COL
VMEM_LIMIT = 12 * 1024 * 1024


def call(body, out_shape, operands, flops, scratch=(), after=()):
    size = sum(a.size * a.dtype.itemsize for a in operands)
    size += sum(s.size * s.dtype.itemsize for s in out_shape)
    count, extra = len(operands), len(after)

    def run(*refs):
        body(*refs[:count], *refs[count + extra :])

    whole = pl.BlockSpec(memory_space=pltpu.VMEM)
    return pl.pallas_call(
        run,
        out_shape=out_shape,
        in_specs=[whole] * count + [pl.BlockSpec(memory_space=pl.ANY)] * extra,
        out_specs=[whole] * len(out_shape),
        scratch_shapes=scratch,
        compiler_params=pltpu.CompilerParams(vmem_limit_bytes=VMEM_LIMIT),
        cost_estimate=pl.CostEstimate(flops=flops, bytes_accessed=size, transcendentals=0),
    )(*operands, *after)


def struct(shape, dtype):
    return jax.ShapeDtypeStruct(shape, dtype)


def unit_rows(values):
    wide = values.astype(F32)
    length = jnp.sqrt(jnp.sum(wide * wide, axis=-1, keepdims=True) + 1e-06)
    return (wide / length, length)


def split3(e):
    high = e.astype(BF16).astype(F32)
    mid = (e - high).astype(BF16).astype(F32)
    low = e - high - mid
    row = lax.broadcasted_iota(jnp.int32, (TILE, LANES), 0)
    parts = jnp.where(row == 0, high, jnp.where(row == 1, mid, jnp.where(row == 2, low, 0.0)))
    return parts.astype(BF16)


def join3(parts):
    return jnp.sum(parts.astype(F32), axis=0, keepdims=True)


def units_kernel(x_ref, unit_ref):
    unit_ref[...] = jnp.broadcast_to(unit_rows(x_ref[...])[0].astype(BF16), unit_ref.shape)


def nt(left, right):
    return lax.dot_general(left, right, (((1,), (1,)), ((), ())), preferred_element_type=F32)


def turned(ring_ref, flip):
    part = ring_ref.shape[1] // NY
    begin = lax.axis_index("y") * part // LANES * LANES
    rest = pl.multiple_of(lax.axis_index("y") * part - begin, TILE)
    flip[...] = ring_ref[:, pl.ds(pl.multiple_of(begin, LANES), 2 * LANES)].T
    return flip[pl.ds(rest, part)]


def split_rows(sums, axis, keep_ref, give_ref):
    rows = keep_ref.shape[0]
    here = lax.axis_index(axis)
    keep_ref[...] = sums[pl.ds(pl.multiple_of(here * rows, TILE), rows)]
    give_ref[...] = sums[pl.ds(pl.multiple_of((1 - here) * rows, TILE), rows)].astype(BF16)


def teacher_kernel(ring_ref, keep_ref, give_ref, flip, upper):
    y = lax.axis_index("y")
    count = ring_ref.shape[1] // LANES
    for i, block in ((0, y), (1, jnp.minimum(count - y, count - 1))):
        begin = pl.multiple_of(block * LANES, LANES)
        flip[i * LANES : (i + 1) * LANES] = ring_ref[:, pl.ds(begin, LANES)].T
    for k in range(count):
        first = k < count - y
        row_block = jnp.where(first, y, count - y)
        col_block = jnp.where(first, y + k, k)
        used = jnp.logical_or(first, 2 * y < count)
        col_block = jnp.where(used, col_block, 0)
        weight = jnp.where(used, jnp.where(row_block == col_block, 1.0, 2.0**0.5), 0.0)
        left = flip[pl.ds(pl.multiple_of(jnp.where(first, 0, LANES), LANES), LANES)]
        right = ring_ref[:, pl.ds(pl.multiple_of(col_block * LANES, LANES), LANES)]
        block = jnp.dot(left, right, preferred_element_type=F32)
        upper[k * LANES : (k + 1) * LANES] = weight * block
    split_rows(upper, "z1", keep_ref, give_ref)


def student_kernel(ring_s, ring_t, give_ref, flip):
    width = ring_s.shape[1]
    quad, rows = give_ref.shape[:2]
    part = quad * rows
    left = turned(ring_s, flip)
    ss = jnp.dot(left, ring_s[...], preferred_element_type=F32)
    row = lax.broadcasted_iota(jnp.int32, (part, width), 0) + lax.axis_index("y") * part
    on = row == lax.broadcasted_iota(jnp.int32, (part, width), 1)
    ss = ss - jnp.where(on, ring_s.shape[0] / width, 0.0)
    st = -jnp.dot(left, ring_t[...], preferred_element_type=F32)
    for at, sums in ((0, ss), (width, st)):
        for i in range(quad):
            give_ref[i, :, at : at + width] = sums[i * rows : (i + 1) * rows].astype(BF16)


def quad_kernel(got_ref, total_ref, send_ref):
    total = jnp.sum(got_ref[...].astype(F32), axis=0)
    total_ref[...] = total
    send_ref[...] = total.astype(BF16)


def halve_kernel(mine_ref, got_ref, keep_ref, give_ref, sums):
    sums[...] = mine_ref[...] + got_ref[...].astype(F32)
    split_rows(sums, "z2", keep_ref, give_ref)


def energy_kernel(mine_ref, got_ref, e_ref):
    tt = mine_ref[...] + got_ref[...].astype(F32)
    e_ref[...] = jnp.broadcast_to(jnp.sum(tt * tt, axis=0, keepdims=True), e_ref.shape)


def energies_kernel(e_ref, out_ref):
    out_ref[...] = jnp.broadcast_to(jnp.sum(e_ref[...], axis=0), out_ref.shape)


def add_kernel(mine_ref, got_ref, total_ref, send_ref):
    total = mine_ref[...] + got_ref[...].astype(F32)
    total_ref[...] = total
    send_ref[...] = total.astype(BF16)


def exchange_kernel(mine_ref, got_ref, out_ref):
    out_ref[...] = jnp.broadcast_to(
        (mine_ref[...] + got_ref[...].astype(F32)).astype(BF16), out_ref.shape
    )


def pull_kernel(whole, ring_s, ring_t, e_ref, f_ref, out_ref):
    part, width = whole.shape[0], whole.shape[1] // 2
    pull = nt(whole[:, :width], ring_s[...]) + nt(whole[:, width:], ring_t[...])
    parts = split3(e_ref[0:1] + f_ref[0:1])
    n = out_ref.shape[2]
    for i in range(NY):
        out_ref[i, 0:part] = pull[:, i * n : (i + 1) * n].astype(BF16)
        out_ref[i, part:] = parts


def finish_kernel(scale, diag, blocks_ref, student_ref, out_ref):
    n, width = student_ref.shape
    part = width // NY
    parts = sum(join3(blocks_ref[i, part:]) for i in range(NY))
    energy = jnp.sum(parts, axis=1, keepdims=True)
    factor = scale / energy
    unit_f, norm_s = unit_rows(student_ref[...])
    pull_t = jnp.concatenate([blocks_ref[i, 0:part].astype(F32) for i in range(NY)], axis=0)
    pull = (pull_t.T + diag * unit_f.astype(BF16).astype(F32)) * factor
    along = jnp.sum(pull * unit_f, axis=-1, keepdims=True)
    out_ref[...] = (pull - along * unit_f) / norm_s


def swap(x, axis):
    return lax.ppermute(x, axis, [(0, 1), (1, 0)])


def gather_y(x):
    n, width = x.shape
    (copies,) = call(units_kernel, [struct((NY, n, width), BF16)], [x], 5 * n * width)
    return lax.all_to_all(copies, "y", 0, 0).reshape(NY * n, width)


def on_device(student, teacher):
    n, width = student.shape
    batch_texts = n * lax.axis_size(COL)
    total_texts = n * lax.axis_size(ALL)
    part = width // NY
    rows = part // 4
    texts = n * NY
    mac = texts * part * width

    def pair(rows, wide):
        return [struct((rows, wide), F32), struct((rows, wide), BF16)]

    ring_t = gather_y(teacher)
    ring_s = gather_y(student)

    quad = ("z2", "z1")
    tt, tt_give = call(
        teacher_kernel,
        pair(width // 2, LANES),
        [ring_t],
        mac,
        [pltpu.VMEM((2 * LANES, texts), BF16), pltpu.VMEM((width, LANES), F32)],
    )
    tt_got = swap(tt_give, "z1")
    tt, tt_give = call(
        halve_kernel,
        pair(width // 4, LANES),
        [tt, tt_got],
        part * width,
        [pltpu.VMEM((width // 2, LANES), F32)],
    )
    tt_got = swap(tt_give, "z2")
    z2_give = tt_give
    tt, tt_give = call(add_kernel, pair(width // 4, LANES), [tt, tt_got], rows * width)
    (give,) = call(
        student_kernel,
        [struct((4, rows, 2 * width), BF16)],
        [ring_s, ring_t],
        4 * mac,
        [pltpu.VMEM((2 * LANES, texts), BF16)],
    )
    give = lax.optimization_barrier((give, z2_give))[0]
    tt_got = swap(tt_give, "zf")
    got = lax.all_to_all(give, quad, 0, 0)
    keep, give = call(
        quad_kernel, pair(rows, 2 * width), [got], 4 * rows * width, after=[tt_got]
    )
    got = swap(give, "zf")
    some = ("xc", "z2", "z1")
    (e,) = call(
        energy_kernel,
        [struct((lax.axis_size(some), 1, LANES), F32)],
        [tt, tt_got],
        3 * rows * width,
        after=[give],
    )
    e = lax.all_to_all(e, some, 0, 0)
    (mine,) = call(
        exchange_kernel,
        [struct((4, rows, 2 * width), BF16)],
        [keep, got],
        2 * rows * width,
        after=[e],
    )
    whole = lax.all_to_all(mine, quad, 0, 0).reshape(part, 2 * width)
    (e,) = call(energies_kernel, [struct((8, LANES), F32)], [e], e.size, after=[mine])
    e_far = swap(e, "zh")
    (blocks,) = call(
        pull_kernel,
        [struct((NY, part + TILE, n), BF16)],
        [whole, ring_s, ring_t, e, e_far],
        4 * mac,
    )
    blocks = lax.all_to_all(blocks, "y", 0, 0)
    (out,) = call(
        functools.partial(finish_kernel, batch_texts**0.5 * total_texts, batch_texts / width),
        [struct((n, width), F32)],
        [blocks, student],
        12 * n * width,
    )
    return out


def solution(mesh):
    rows, cols = mesh.devices.shape
    fine = Mesh(mesh.devices.reshape(2, rows // 2, 2, 2, 2, cols // NZ), ALL)
    return jax.shard_map(
        on_device,
        mesh=fine,
        in_specs=(P(ALL, None), P(ALL, None)),
        out_specs=P(ALL, None),
        check_vma=False,
    )
```
